512 devices in a mesh: col: 128 (over x, z, y_hi), rep: 4 (over y_lo, core).
Axes of the slice: x: 4, y: 8 (y_hi: 4, y_lo: 2; y = y_hi * 2 + y_lo), z: 8, core: 2. Of those that a mesh axis runs over, the one named last changes fastest.
Arguments:
- tokens: bfloat16 [327680, 768], P(('col', 'rep')), may hold values from -6 to 6
- lengths: int32 [1024], P(('col', 'rep')), may hold values from 1 to 512, as said below
- partner: int32 [1024], P(('col', 'rep')), may hold values from 0 to 1023, as said below
- w_query: bfloat16 [768, 384], replicated, may hold values from -1 to 1
- w_keyval: bfloat16 [768, 768], replicated, may hold values from -1 to 1
- w_output: bfloat16 [384, 768], replicated, may hold values from -0.3125 to 0.3125
Outputs:
- col_loss: float32 [1024], P(('col', 'rep'))
- keyval_grad: float32 [768, 768], P('rep')
The draws below stay inside these ranges and needn't reach their ends.
Inputs may be any that keep to these rules, and one draw needn't show every extreme that they name: In each block of 2 columns the lengths sum to at most 640; some block sums to exactly 640, and some column has exactly 512 tokens. Columns come in pairs: partner of partner of a column is the column itself, and no column is its own partner.
All inputs are finite; a program needn't handle non-finite values.
Results may differ from the reference program's by a relative error of at most 0.015.
Values may be sent and summed in bfloat16 or wider, within the bound.
A program may use at most 64 MiB of HBM per device.

```python
import jax
import jax.numpy as jnp
from jax import lax

D = 768
HEAD = 64
NHEAD = 6
LMAX = 512
COL_DEV = 2
TOK_DEV = 640
COLUMNS = 1024
TOKENS = 327680


def draw_lengths(key, part):
    nblocks = COLUMNS // COL_DEV
    first, second = jax.random.split(jax.random.fold_in(key, 11))
    raw = jax.random.randint(first, (nblocks, COL_DEV), 1, LMAX + 1, dtype=jnp.int32)
    total = jnp.sum(raw, axis=1, keepdims=True)
    shrunk = raw * (TOK_DEV - COL_DEV) // total + 1
    fitted = jnp.where(total > TOK_DEV, shrunk, raw)
    chosen = jax.random.randint(second, (), 0, nblocks, dtype=jnp.int32)
    place = jnp.arange(COL_DEV, dtype=jnp.int32)
    spare = TOK_DEV - LMAX
    share = spare // (COL_DEV - 1)
    leftover = spare % (COL_DEV - 1)
    pattern = jnp.where(place == 0, LMAX, share + jnp.where(place == COL_DEV - 1, leftover, 0)).astype(jnp.int32)
    blockid = jnp.arange(nblocks, dtype=jnp.int32)
    fitted = jnp.where(blockid[:, None] == chosen, pattern[None, :], fitted)
    return fitted.reshape(-1).astype(jnp.int32)


def draw_partner(key, part):
    order = jax.random.permutation(jax.random.fold_in(key, 23), COLUMNS).astype(jnp.int32)
    swapped = order.reshape(-1, 2)[:, ::-1].reshape(-1)
    result = jnp.zeros((COLUMNS,), jnp.int32).at[order].set(swapped)
    return result.astype(jnp.int32)


def projection_base(key):
    raw = jax.random.normal(jax.random.fold_in(key, 31), (D, NHEAD * HEAD), jnp.float32)
    return jnp.clip(raw, -6.0, 6.0) * D ** (-0.5)


def draw_w_query(key, part):
    return projection_base(key).astype(jnp.bfloat16)


def draw_w_keyval(key, part):
    raw = jax.random.normal(jax.random.fold_in(key, 37), (D, 2 * NHEAD * HEAD), jnp.float32)
    fresh = jnp.clip(raw, -6.0, 6.0) * D ** (-0.5)
    result = fresh
    return result.astype(jnp.bfloat16)


def draw_tokens(key, part):
    nblocks = COLUMNS // COL_DEV
    drawn = jnp.clip(jax.random.normal(jax.random.fold_in(key, 41), (nblocks, TOK_DEV, D), jnp.float32), -6.0, 6.0)
    spans = draw_lengths(key, part).reshape(nblocks, COL_DEV)
    starts = jnp.cumsum(spans, axis=1, dtype=jnp.int32) - spans
    keep_own = jnp.zeros((COLUMNS,), bool)
    result = drawn
    flat = result.reshape(TOKENS, D)
    partner = draw_partner(key, part)
    columns = jnp.arange(COLUMNS, dtype=jnp.int32)
    pair_id = jnp.minimum(columns, partner)
    table = jnp.clip(jax.random.normal(jax.random.fold_in(key, 59), (COLUMNS, D), jnp.float32), -6.0, 6.0)
    shared = table[pair_id]
    pair_level = jax.random.uniform(jax.random.fold_in(key, 61), (COLUMNS,), jnp.float32, 0.0, 0.97)[pair_id]
    nclusters = max(COLUMNS // 8, 1)
    cluster_of = jax.random.randint(jax.random.fold_in(key, 67), (COLUMNS,), 0, nclusters, dtype=jnp.int32)[pair_id]
    cluster_table = jnp.clip(jax.random.normal(jax.random.fold_in(key, 71), (nclusters, D), jnp.float32), -6.0, 6.0)
    cluster_level = jax.random.uniform(jax.random.fold_in(key, 73), (nclusters,), jnp.float32, 0.0, 0.95)[cluster_of]
    grouped = cluster_table[cluster_of]
    first_index = (jnp.arange(nblocks, dtype=jnp.int32)[:, None] * TOK_DEV + starts).reshape(-1)
    own = flat[first_index]
    weight_cluster = jnp.sqrt(cluster_level)[:, None]
    weight_pair = jnp.sqrt(pair_level * (1.0 - cluster_level))[:, None]
    weight_own = jnp.sqrt((1.0 - pair_level) * (1.0 - cluster_level))[:, None]
    blended = jnp.clip(weight_cluster * grouped + weight_pair * shared + weight_own * own, -6.0, 6.0)
    blended = jnp.where(keep_own[:, None], own, blended)
    flat = flat.at[first_index].set(blended)
    return flat.astype(jnp.bfloat16)


def centred(rng, dims, deviation, limit, kind=jnp.bfloat16):
    drawn = jax.random.normal(rng, dims, jnp.float32) * deviation
    return jnp.minimum(jnp.maximum(drawn, -limit), limit).astype(kind)


def setup_inputs(seed: int = 0) -> dict:
    arg_keys = jax.random.split(jax.random.key(seed), 7)
    return {
        "tokens": draw_tokens(jax.random.fold_in(arg_keys[6], 71), 0),
        "lengths": draw_lengths(jax.random.fold_in(arg_keys[6], 71), 0),
        "partner": draw_partner(jax.random.fold_in(arg_keys[6], 71), 0),
        "w_query": draw_w_query(jax.random.fold_in(arg_keys[6], 71), 0),
        "w_keyval": draw_w_keyval(jax.random.fold_in(arg_keys[6], 71), 0),
        "w_output": centred(arg_keys[5], (NHEAD * HEAD, D), (NHEAD * HEAD) ** -0.5, 0.3125),
    }


sharpness_divisor = 0.07

def project(tokens, w_keyval):
    return jnp.dot(tokens, w_keyval, preferred_element_type=jnp.float32).astype(jnp.bfloat16)

def attend(keyval, tokens, lengths, w_query, w_output):
    rows = tokens.shape[0]
    count = lengths.shape[0]
    width = w_query.shape[1]
    heads = width // HEAD
    starts = jnp.cumsum(lengths, dtype=jnp.int32) - lengths
    place = jnp.arange(rows, dtype=jnp.int32)
    member = (place[None, :] >= starts[:, None]) & (place[None, :] < (starts + lengths)[:, None])
    first_rows = jnp.take(tokens, starts, axis=0)
    query = jnp.dot(first_rows, w_query, preferred_element_type=jnp.float32).astype(jnp.bfloat16)
    query = query.reshape(count, heads, HEAD)
    keys = keyval[:, :width].reshape(rows, heads, HEAD)
    values = keyval[:, width:].reshape(rows, heads, HEAD)
    scores = jnp.einsum('chd,thd->cht', query.astype(jnp.float32), keys.astype(jnp.float32)) * HEAD ** (-0.5)
    scores = jnp.where(member[:, None, :], scores, -1e+30)
    peak = lax.optimization_barrier(jnp.max(scores, axis=2, keepdims=True))
    lifted = jnp.exp(scores - peak)
    weights = (lifted / lax.optimization_barrier(jnp.sum(lifted, axis=2, keepdims=True))).astype(jnp.bfloat16)
    mixed = jnp.einsum('cht,thd->chd', weights.astype(jnp.float32), values.astype(jnp.float32))
    mixed = mixed.reshape(count, width).astype(jnp.bfloat16)
    return first_rows.astype(jnp.float32) + jnp.dot(mixed, w_output, preferred_element_type=jnp.float32)

def reference(tokens, lengths, partner, w_query, w_keyval, w_output):
    nblocks = COLUMNS // COL_DEV
    blocks = tokens.reshape(nblocks, TOK_DEV, D)
    spans = lengths.reshape(nblocks, COL_DEV)

    def encode(pair):
        rows, span = pair
        return attend(project(rows, w_keyval), rows, span, w_query, w_output)
    embed = lax.map(encode, (blocks, spans)).reshape(COLUMNS, D)
    norm = jnp.sqrt(lax.optimization_barrier(jnp.sum(embed * embed, axis=1, keepdims=True)) + 1e-06)
    unit = embed / norm
    paired_normalized_directions = unit.astype(jnp.bfloat16)
    cosine_score_matrix = jnp.dot(paired_normalized_directions, paired_normalized_directions.T, preferred_element_type=jnp.float32) / sharpness_divisor
    lse = jnp.log(lax.optimization_barrier(jnp.sum(jnp.exp(cosine_score_matrix), axis=1)))
    index = jnp.arange(COLUMNS, dtype=jnp.int32)
    match = index[None, :] == partner[:, None]
    positive = lax.optimization_barrier(jnp.sum(jnp.where(match, cosine_score_matrix, 0.0), axis=1))
    col_loss = lse - positive
    normalized_exponential_shares = jnp.exp(cosine_score_matrix - lse[:, None]).astype(jnp.bfloat16)
    paired_field_encodings = jnp.take(paired_normalized_directions, partner, axis=0).astype(jnp.float32)
    normalized_direction_derivative = (jnp.dot(normalized_exponential_shares, paired_normalized_directions, preferred_element_type=jnp.float32) + jnp.dot(normalized_exponential_shares.T, paired_normalized_directions, preferred_element_type=jnp.float32) - 2.0 * paired_field_encodings) / sharpness_divisor
    radial = lax.optimization_barrier(jnp.sum(unit * normalized_direction_derivative, axis=1, keepdims=True))
    dembed = ((normalized_direction_derivative - unit * radial) / norm).reshape(nblocks, COL_DEV, D)

    def accumulate(total, triple):
        rows, span, cotan = triple
        keyval = project(rows, w_keyval)
        _, pull = jax.vjp(lambda inner: attend(inner, rows, span, w_query, w_output), keyval)
        dkeyval = pull(cotan)[0]
        term = lax.dot_general(rows, dkeyval, (((0,), (0,)), ((), ())), preferred_element_type=jnp.float32)
        return (total + term, None)
    start = jnp.zeros((D, w_keyval.shape[1]), jnp.float32)
    keyval_grad, _ = lax.scan(accumulate, start, (blocks, spans, dembed))
    return (col_loss, keyval_grad)
```

```python
import functools

import jax
import jax.numpy as jnp
from jax import lax
from jax.experimental import pallas as pl
from jax.experimental.pallas import tpu as pltpu
from jax.sharding import PartitionSpec as P

HEAD = 64
SHARP = 0.07
BF = jnp.bfloat16
F32 = jnp.float32
MESH = pl.DeviceIdType.MESH
NX, NY, NZ = 4, 8, 8
NEAR = (1, 7, 2, 6, 3, 5, 4)

XC = [(dx, dk) for dx in range(NX) for dk in range(2) if (dx, dk) != (0, 0)]
XY = [(dx, dh) for dx in range(NX) for dh in range(4) if (dx, dh) != (0, 0)]
PEERS = sorted(
    {(dx, 0, 0, dk) for dx, dk in XC}
    | {(0, j, 0, 0) for j in NEAR}
    | {(0, 0, j, 0) for j in NEAR}
    | {(dx, 2 * dh, 0, 0) for dx, dh in XY}
)


def mm(a, b):
    return jnp.dot(a, b, preferred_element_type=F32)


def mm_t(a, b):
    return lax.dot_general(a, b, (((1,), (1,)), ((), ())), preferred_element_type=F32)


def mm_tl(a, b):
    return lax.dot_general(a, b, (((0,), (0,)), ((), ())), preferred_element_type=F32)


def two(a):
    high = a.astype(BF)
    low = (a - high.astype(F32)).astype(BF)
    return jnp.concatenate([high, low], axis=0)


def fold(a):
    return a[:16] + a[16:]


def device(x, y, z, k):
    return ((x * NZ + z) * 4 + y // 2, lax.rem(y, 2) * 2 + k)


def kernel(
    lens, part, tok, wq, wkv, wo,
    loss_out, grad_out,
    a1_s, a1_r, u, tperm, early_s, early_r, late_s, late_r, r2_s, r2_r, r3_r, ag_r,
    soft, a1_ss, a1_rs, a2_ss, a2_rs, a3_ss, a3_rs, fw_ss, fw_rs,
    e_ss, e_rs, l_ss, l_rs, r2_ss, r2_rs, r3_ss, r3_rs, ag_ss, ag_rs,
):
    col, rep = lax.axis_index("col"), lax.axis_index("rep")
    x, z = col // 32, lax.rem(col // 4, 8)
    yh, yl, k = lax.rem(col, 4), rep // 2, lax.rem(rep, 2)
    y = yh * 2 + yl
    m = x * 2 + k

    def at(dx, dy, dz, dk):
        return (
            lax.rem(x + dx, NX), lax.rem(y + dy, NY), lax.rem(z + dz, NZ), lax.rem(k + dk, 2)
        )

    def remote(src, dst, ss, rs, place):
        return pltpu.make_async_remote_copy(
            src_ref=src, dst_ref=dst, send_sem=ss, recv_sem=rs,
            device_id=device(*place), device_id_type=MESH,
        )

    barrier = pltpu.get_barrier_semaphore()
    for off in PEERS:
        pl.semaphore_signal(
            barrier, inc=1, device_id=device(*at(*off)), device_id_type=MESH
        )

    row = lax.broadcasted_iota(jnp.int32, (16, 640), 0)
    pos = lax.broadcasted_iota(jnp.int32, (16, 640), 1)
    l0, l1 = lens[0], lens[1]
    lo = jnp.where(row < 8, 0, l0)
    hi = jnp.where(row < 8, l0, l0 + l1)
    t = tok[...]
    first = mm((pos == lo).astype(F32).astype(BF), t)
    hrow = lax.rem(lax.broadcasted_iota(jnp.int32, (16, 384), 0), 8)
    own_head = lax.broadcasted_iota(jnp.int32, (16, 384), 1) // HEAD == hrow
    query = mm(first.astype(BF), wq[...]).astype(BF).astype(F32)
    qexp = jnp.where(own_head, query, 0.0).astype(BF)
    wk, wv = wkv[:, :384], wkv[:, 384:]
    scores = fold(mm_t(two(mm_t(qexp, wk)), t)) * HEAD ** (-0.5)
    scores = jnp.where((pos >= lo) & (pos < hi), scores, -1e30)
    lifted = jnp.exp(scores - jnp.max(scores, axis=1, keepdims=True))
    weights = lifted / jnp.sum(lifted, axis=1, keepdims=True)
    soft[...] = weights
    wb = weights.astype(BF)
    pooled = mm(wb, t)
    mixed = jnp.where(own_head, fold(mm(two(pooled), wv)), 0.0)
    mixed = jnp.sum(mixed.reshape(2, 8, 384), axis=1, keepdims=True)
    mixed = jnp.broadcast_to(mixed, (2, 8, 384)).reshape(16, 384).astype(BF)
    embed = first + mm(mixed, wo[...])
    norm = jnp.sqrt(jnp.sum(embed * embed, axis=1, keepdims=True) + 1e-06)
    unit = embed / norm
    unit_b = unit.astype(BF)
    ub = unit_b.astype(F32)
    row16 = lax.broadcasted_iota(jnp.int32, (16, 768), 0)
    placed = jnp.where(row16 == 2 * m, ub[0:1], jnp.where(row16 == 2 * m + 1, ub[8:9], 0.0))
    placed = placed.astype(BF)
    a1_s[0] = placed[:, :384]
    a1_s[1] = placed[:, 384:]

    pl.semaphore_wait(barrier, len(PEERS))

    def group_copies(src, dst, ss, rs):
        copies = []
        for dx, dk in XC:
            place = at(dx, 0, 0, dk)
            slot = dx * 2 + dk
            copies.append(remote(src(place), dst.at[slot], ss.at[slot], rs.at[slot], place))
        return copies

    a1 = group_copies(lambda p: a1_s.at[p[3]], a1_r, a1_ss, a1_rs)
    for cp in a1:
        cp.start()

    lane = lax.broadcasted_iota(jnp.int32, (768, 128), 1)
    deep = lax.broadcasted_iota(jnp.int32, (768, 128), 0)
    py, pv = lane // 16, lax.rem(lane, 16)
    base = lax.rem(py, 2) * 384 + (py // 2) * 12 + pv
    base = jnp.where(pv < 12, base, 100000)

    def permute(i):
        want = base + ((i % 2) * 192 + (i // 2) * 48)
        pick = (deep == want).astype(F32).astype(BF)
        tperm[i] = mm(tok[...], pick).astype(BF)

    for i in range(2):
        permute(i)
    for cp in a1:
        cp.wait_recv()
    block = a1_s[k].astype(F32)
    for s in range(1, 8):
        block = block + a1_r[s].astype(F32)
    block = block.astype(BF)

    def gather(half):
        lanes = slice(half * 384, half * 384 + 384)
        u[z, y, :, lanes] = block
        mine = u.at[z, y, :, lanes]

        def line(j, second):
            along_z = (half == 0) == second
            return at(0, 0, j, 0) if along_z else at(0, j, 0, 0)

        def plane(j):
            p = at(0, 8 - j, 8 - j, 0)
            return u.at[p[2], :, :, lanes] if half == 0 else u.at[:, p[1], :, lanes]

        own = u.at[z, :, :, lanes] if half == 0 else u.at[:, y, :, lanes]
        a2 = [remote(mine, mine, a2_ss.at[j], a2_rs.at[j], line(j, False)) for j in NEAR]
        for cp in a2:
            cp.start()
        for i in range(2, 8):
            permute(i)
        for cp in a2:
            cp.wait_recv()
        a3 = [remote(own, own, a3_ss.at[j], a3_rs.at[j], line(j, True)) for j in NEAR]
        for cp in a3:
            cp.start()
        fw = []
        for n, j in enumerate((0,) + NEAR):
            if n:
                a3[n - 1].wait_recv()
            reg = own if j == 0 else plane(j)
            cp = remote(reg, reg, fw_ss.at[j], fw_rs.at[j], at(0, 0, 0, 1))
            cp.start()
            fw.append(cp)
            if n == 0:
                for i in range(8):
                    early_s[i, :, 0:128] = mm(wb, tperm[i]).astype(BF)
                    early_s[i, :, 128:512] = qexp
                e = group_copies(lambda p: early_s.at[p[0] * 2 + p[3]], early_r, e_ss, e_rs)
                for cp in e:
                    cp.start()
        for cp in fw:
            cp.wait_recv()
        for cp in a2 + a3 + fw:
            cp.wait_send()
        for cp in e:
            cp.wait()

    pl.when(k == 0)(functools.partial(gather, 0))
    pl.when(k == 1)(functools.partial(gather, 1))
    for cp in a1:
        cp.wait_send()

    scale = 1.0 / SHARP
    total = jnp.zeros((1, 1024), F32)
    whole = u[...].reshape(1024, 768)
    for i in range(4):
        part_s = mm_t(u[2 * i : 2 * i + 2].reshape(256, 768), whole)
        total = total + jnp.sum(jnp.exp(part_s * scale), axis=0, keepdims=True)
    all_lse = jnp.log(total)
    logits = mm_t(unit_b, whole) * scale
    lse = jnp.log(jnp.sum(jnp.exp(logits), axis=1, keepdims=True))
    n = lax.broadcasted_iota(jnp.int32, (16, 1024), 1)
    nz, ny, nm, nc = n // 128, lax.rem(n // 16, 8), lax.rem(n // 2, 8), lax.rem(n, 2)
    number = (((nm // 2) * 8 + nz) * 4 + ny // 2) * 4 + lax.rem(ny, 2) * 2 + lax.rem(nm, 2)
    number = number * 2 + nc
    lrow = lax.broadcasted_iota(jnp.int32, (16, 1024), 0)
    match = number == jnp.where(lrow < 8, part[0], part[1])
    positive = jnp.sum(jnp.where(match, logits, 0.0), axis=1, keepdims=True)
    loss_out[...] = jnp.broadcast_to(lse - positive, (16, 128))
    rowp = jnp.exp(logits - lse).astype(BF)
    colp = jnp.exp(logits - all_lse).astype(BF)
    stack = jnp.concatenate([rowp, colp, match.astype(F32).astype(BF)], axis=0)
    terms = mm(stack, whole)
    dunit = (terms[:16] + terms[16:32] - 2.0 * terms[32:]) / SHARP
    radial = jnp.sum(unit * dunit, axis=1, keepdims=True)
    dembed = (dunit - unit * radial) / norm

    dmixed = fold(mm_t(two(dembed), wo[...])).astype(BF).astype(F32)
    dmexp = jnp.where(own_head, dmixed, 0.0).astype(BF)
    dweights = fold(mm_t(two(mm_t(dmexp, wv)), t)).astype(BF).astype(F32)
    weights = soft[...]
    dscores = weights * (dweights - jnp.sum(weights * dweights, axis=1, keepdims=True))
    ds2 = two(dscores * HEAD ** (-0.5))
    for i in range(8):
        late_s[i, :, 0:128] = fold(mm(ds2, tperm[i])).astype(BF)
        late_s[i, :, 128:512] = dmexp
    late = group_copies(lambda p: late_s.at[p[0] * 2 + p[3]], late_r, l_ss, l_rs)
    for cp in late:
        cp.start()
    early_r[0] = early_s[m]
    late_r[0] = late_s[m]
    for cp in late:
        cp.wait_recv()

    keys = mm_tl(late_r[:, :, 0:128].reshape(128, 128), early_r[:, :, 128:512].reshape(128, 384))
    vals = mm_tl(early_r[:, :, 0:128].reshape(128, 128), late_r[:, :, 128:512].reshape(128, 384))
    r2_s[:, :, 0:384] = keys.astype(BF).reshape(8, 16, 384)
    r2_s[:, :, 384:768] = vals.astype(BF).reshape(8, 16, 384)
    r2 = []
    for j in NEAR:
        place = at(0, j, 0, 0)
        cp = remote(r2_s.at[place[1]], r2_r.at[j], r2_ss.at[j], r2_rs.at[j], place)
        cp.start()
        r2.append(cp)
    sum2 = r2_s[y].astype(F32)
    for cp, j in zip(r2, NEAR):
        cp.wait_recv()
        sum2 = sum2 + r2_r[j].astype(F32)
    r3_r[z] = sum2.astype(BF)
    r3 = []
    for j in NEAR:
        cp = remote(r3_r.at[z], r3_r.at[z], r3_ss.at[j], r3_rs.at[j], at(0, 0, j, 0))
        cp.start()
        r3.append(cp)
    for cp in r3:
        cp.wait_recv()
    sum3 = r3_r[0].astype(F32)
    for j in range(1, 8):
        sum3 = sum3 + r3_r[j].astype(F32)
    mine = x * 4 + yh
    ag_r[mine] = sum3.astype(BF)
    ag = []
    for dx, dh in XY:
        cp = remote(
            ag_r.at[mine], ag_r.at[mine], ag_ss.at[dx * 4 + dh], ag_rs.at[dx * 4 + dh],
            at(dx, 2 * dh, 0, 0),
        )
        cp.start()
        ag.append(cp)
    for cp in ag:
        cp.wait_recv()
    for i in range(16):
        grad_out[12 * i : 12 * i + 12, :] = ag_r[i].astype(F32)[0:12]
    for cp in late + r2 + r3 + ag:
        cp.wait_send()


def per_device(tokens, lengths, partner, w_query, w_keyval, w_output):
    smem = pl.BlockSpec(memory_space=pltpu.SMEM)
    vmem = pl.BlockSpec(memory_space=pltpu.VMEM)
    dma = pltpu.SemaphoreType.DMA
    loss, grad = pl.pallas_call(
        kernel,
        name="contrast",
        out_shape=(
            jax.ShapeDtypeStruct((16, 128), F32),
            jax.ShapeDtypeStruct((192, 768), F32),
        ),
        in_specs=[smem, smem, vmem, vmem, vmem, vmem],
        out_specs=(vmem, vmem),
        scratch_shapes=[
            pltpu.VMEM((2, 16, 384), BF),
            pltpu.VMEM((8, 16, 384), BF),
            pltpu.VMEM((8, 8, 16, 768), BF),
            pltpu.VMEM((8, 640, 128), BF),
            pltpu.VMEM((8, 16, 512), BF),
            pltpu.VMEM((8, 16, 512), BF),
            pltpu.VMEM((8, 16, 512), BF),
            pltpu.VMEM((8, 16, 512), BF),
            pltpu.VMEM((8, 16, 768), BF),
            pltpu.VMEM((8, 16, 768), BF),
            pltpu.VMEM((8, 16, 768), BF),
            pltpu.VMEM((16, 16, 768), BF),
            pltpu.VMEM((16, 640), F32),
        ]
        + [dma((8,))] * 16
        + [dma((16,))] * 2,
        compiler_params=pltpu.CompilerParams(
            collective_id=0, has_side_effects=True, vmem_limit_bytes=48 * 2**20
        ),
    )(lengths, partner, tokens, w_query, w_keyval, w_output)
    return loss[::8, 0], grad


def solution(mesh):
    in_specs = (P(("col", "rep"), None), P(("col", "rep")), P(("col", "rep")), P(), P(), P())
    out_specs = (P(("col", "rep")), P("rep", None))
    return jax.shard_map(
        per_device, mesh=mesh, in_specs=in_specs, out_specs=out_specs, check_vma=False
    )
```

```python
import functools

import jax
import jax.numpy as jnp
from jax import lax
from jax.experimental import pallas as pl
from jax.experimental.pallas import tpu as pltpu
from jax.sharding import PartitionSpec as P

HEAD = 64
SHARP = 0.07
BF = jnp.bfloat16
F32 = jnp.float32
MESH = pl.DeviceIdType.MESH
NX, NY, NZ = 4, 8, 8
NEAR = (1, 7, 2, 6, 3, 5, 4)

XC = [(dx, dk) for dx in range(NX) for dk in range(2) if (dx, dk) != (0, 0)]
XZ = [(dx, dz) for dx in range(NX) for dz in (0,) + NEAR if (dx, dz) != (0, 0)]
PEERS = sorted(
    {(dx, 0, 0, dk) for dx, dk in XC}
    | {(0, j, 0, 0) for j in NEAR}
    | {(0, 0, j, 0) for j in NEAR}
    | {(dx, 0, dz, 0) for dx, dz in XZ}
)


def mm(a, b):
    return jnp.dot(a, b, preferred_element_type=F32)


def mm_t(a, b):
    return lax.dot_general(a, b, (((1,), (1,)), ((), ())), preferred_element_type=F32)


def mm_tl(a, b):
    return lax.dot_general(a, b, (((0,), (0,)), ((), ())), preferred_element_type=F32)


def two(a):
    high = a.astype(BF)
    low = (a - high.astype(F32)).astype(BF)
    return jnp.concatenate([high, low], axis=0)


def fold(a):
    return a[:16] + a[16:]


def device(x, y, z, k):
    return ((x * NZ + z) * 4 + y // 2, lax.rem(y, 2) * 2 + k)


def kernel(
    lens_h, part_h, tok_h, wq_h, wkv_h, wo_h,
    loss_out, grad_out,
    lens, part, tok, wq, wkv, wo, in_s,
    a1_s, a1_r, u, tperm, early_s, early_r, late_s, late_r, r2_s, r2_r, r3_s, r3_r, ag_r,
    soft, a1_ss, a1_rs, a2_ss, a2_rs, a3_ss, a3_rs, fw_ss, fw_rs,
    e_ss, e_rs, l_ss, l_rs, r2_ss, r2_rs, r3_ss, r3_rs, ag_ss, ag_rs,
):
    col, rep = lax.axis_index("col"), lax.axis_index("rep")
    x, z = col // 32, lax.rem(col // 4, 8)
    yh, yl, k = lax.rem(col, 4), rep // 2, lax.rem(rep, 2)
    y = yh * 2 + yl
    m = x * 2 + k

    def at(dx, dy, dz, dk):
        return (
            lax.rem(x + dx, NX), lax.rem(y + dy, NY), lax.rem(z + dz, NZ), lax.rem(k + dk, 2)
        )

    def remote(src, dst, ss, rs, place):
        return pltpu.make_async_remote_copy(
            src_ref=src, dst_ref=dst, send_sem=ss, recv_sem=rs,
            device_id=device(*place), device_id_type=MESH,
        )

    loads = [
        pltpu.make_async_copy(src, dst, in_s.at[i])
        for i, (src, dst) in enumerate(
            [(lens_h, lens), (tok_h, tok), (wq_h, wq), (wkv_h, wkv), (wo_h, wo), (part_h, part)]
        )
    ]
    for cp in loads:
        cp.start()
    barrier = pltpu.get_barrier_semaphore()
    for off in PEERS:
        pl.semaphore_signal(
            barrier, inc=1, device_id=device(*at(*off)), device_id_type=MESH
        )

    row = lax.broadcasted_iota(jnp.int32, (16, 640), 0)
    pos = lax.broadcasted_iota(jnp.int32, (16, 640), 1)
    loads[0].wait()
    loads[1].wait()
    l0, l1 = lens[0], lens[1]
    lo = jnp.where(row < 8, 0, l0)
    hi = jnp.where(row < 8, l0, l0 + l1)
    t = tok[...]
    first = mm((pos == lo).astype(F32).astype(BF), t)
    hrow = lax.rem(lax.broadcasted_iota(jnp.int32, (16, 384), 0), 8)
    own_head = lax.broadcasted_iota(jnp.int32, (16, 384), 1) // HEAD == hrow
    loads[2].wait()
    query = mm(first.astype(BF), wq[...]).astype(BF).astype(F32)
    qexp = jnp.where(own_head, query, 0.0).astype(BF)
    loads[3].wait()
    wk, wv = wkv[:, :384], wkv[:, 384:]
    scores = fold(mm_t(two(mm_t(qexp, wk)), t)) * HEAD ** (-0.5)
    scores = jnp.where((pos >= lo) & (pos < hi), scores, -1e30)
    lifted = jnp.exp(scores - jnp.max(scores, axis=1, keepdims=True))
    weights = lifted / jnp.sum(lifted, axis=1, keepdims=True)
    soft[...] = weights
    wb = weights.astype(BF)
    pooled = mm(wb, t)
    mixed = jnp.where(own_head, fold(mm(two(pooled), wv)), 0.0)
    mixed = jnp.sum(mixed.reshape(2, 8, 384), axis=1, keepdims=True)
    mixed = jnp.broadcast_to(mixed, (2, 8, 384)).reshape(16, 384).astype(BF)
    loads[4].wait()
    embed = first + mm(mixed, wo[...])
    norm = jnp.sqrt(jnp.sum(embed * embed, axis=1, keepdims=True) + 1e-06)
    unit = embed / norm
    unit_b = unit.astype(BF)
    ub = unit_b.astype(F32)
    row16 = lax.broadcasted_iota(jnp.int32, (16, 768), 0)
    placed = jnp.where(row16 == 2 * m, ub[0:1], jnp.where(row16 == 2 * m + 1, ub[8:9], 0.0))
    placed = placed.astype(BF)
    a1_s[0] = placed[:, :384]
    a1_s[1] = placed[:, 384:]

    pl.semaphore_wait(barrier, len(PEERS))

    def group_copies(src, dst, ss, rs):
        copies = []
        for dx, dk in XC:
            place = at(dx, 0, 0, dk)
            slot = dx * 2 + dk
            copies.append(remote(src(place), dst.at[slot], ss.at[slot], rs.at[slot], place))
        return copies

    a1 = group_copies(lambda p: a1_s.at[p[3]], a1_r, a1_ss, a1_rs)
    for cp in a1:
        cp.start()

    def permute(i):
        lane = lax.broadcasted_iota(jnp.int32, (768, 128), 1)
        deep = lax.broadcasted_iota(jnp.int32, (768, 128), 0)
        pz, pl_, pv = lane // 16, lax.rem(lane // 8, 2), lax.rem(lane, 8)
        want = pl_ * 384 + pz * 6 + pv + ((i % 2) * 192 + (i // 2) * 48)
        pick = ((deep == want) & (pv < 6)).astype(F32).astype(BF)
        tperm[i] = mm(tok[...], pick).astype(BF)

    for cp in a1:
        cp.wait_recv()
    block = a1_s[k].astype(F32)
    for s in range(1, 8):
        block = block + a1_r[s].astype(F32)
    block = block.astype(BF)

    def gather(half):
        lanes = slice(half * 384, half * 384 + 384)
        u[z, y, :, lanes] = block
        mine = u.at[z, y, :, lanes]

        def line(j, second):
            along_z = (half == 0) == second
            return at(0, 0, j, 0) if along_z else at(0, j, 0, 0)

        def plane(j):
            p = at(0, 8 - j, 8 - j, 0)
            return u.at[p[2], :, :, lanes] if half == 0 else u.at[:, p[1], :, lanes]

        own = u.at[z, :, :, lanes] if half == 0 else u.at[:, y, :, lanes]
        a2 = [remote(mine, mine, a2_ss.at[j], a2_rs.at[j], line(j, False)) for j in NEAR]
        for cp in a2:
            cp.start()
        for cp in a2:
            cp.wait_recv()
        a3 = [remote(own, own, a3_ss.at[j], a3_rs.at[j], line(j, True)) for j in NEAR]
        for cp in a3:
            cp.start()
        fw = []
        for n, j in enumerate((0,) + NEAR):
            if n:
                a3[n - 1].wait_recv()
            reg = own if j == 0 else plane(j)
            cp = remote(reg, reg, fw_ss.at[j], fw_rs.at[j], at(0, 0, 0, 1))
            cp.start()
            fw.append(cp)
            if n == 0:
                for i in range(8):
                    permute(i)
                    early_s[i, :, 0:128] = mm(wb, tperm[i]).astype(BF)
                    early_s[i, :, 128:512] = qexp
                e = group_copies(lambda p: early_s.at[p[0] * 2 + p[3]], early_r, e_ss, e_rs)
                for cp in e:
                    cp.start()
        for cp in fw:
            cp.wait_recv()
        for cp in a2 + a3 + fw:
            cp.wait_send()
        for cp in e:
            cp.wait()

    pl.when(k == 0)(functools.partial(gather, 0))
    pl.when(k == 1)(functools.partial(gather, 1))
    for cp in a1:
        cp.wait_send()

    scale = 1.0 / SHARP
    total = jnp.zeros((1, 1024), F32)
    whole = u[...].reshape(1024, 768)
    for i in range(4):
        part_s = mm_t(u[2 * i : 2 * i + 2].reshape(256, 768), whole)
        total = total + jnp.sum(jnp.exp(part_s * scale), axis=0, keepdims=True)
    all_lse = jnp.log(total)
    logits = mm_t(unit_b, whole) * scale
    lse = jnp.log(jnp.sum(jnp.exp(logits), axis=1, keepdims=True))
    n = lax.broadcasted_iota(jnp.int32, (16, 1024), 1)
    nz, ny, nm, nc = n // 128, lax.rem(n // 16, 8), lax.rem(n // 2, 8), lax.rem(n, 2)
    number = (((nm // 2) * 8 + nz) * 4 + ny // 2) * 4 + lax.rem(ny, 2) * 2 + lax.rem(nm, 2)
    number = number * 2 + nc
    lrow = lax.broadcasted_iota(jnp.int32, (16, 1024), 0)
    loads[5].wait()
    match = number == jnp.where(lrow < 8, part[0], part[1])
    positive = jnp.sum(jnp.where(match, logits, 0.0), axis=1, keepdims=True)
    loss_out[...] = jnp.broadcast_to(lse - positive, (16, 128))
    rowp = jnp.exp(logits - lse).astype(BF)
    colp = jnp.exp(logits - all_lse).astype(BF)
    stack = jnp.concatenate([rowp, colp, match.astype(F32).astype(BF)], axis=0)
    terms = mm(stack, whole)
    dunit = (terms[:16] + terms[16:32] - 2.0 * terms[32:]) / SHARP
    radial = jnp.sum(unit * dunit, axis=1, keepdims=True)
    dembed = (dunit - unit * radial) / norm

    dmixed = fold(mm_t(two(dembed), wo[...])).astype(BF).astype(F32)
    dmexp = jnp.where(own_head, dmixed, 0.0).astype(BF)
    dweights = fold(mm_t(two(mm_t(dmexp, wv)), t)).astype(BF).astype(F32)
    weights = soft[...]
    dscores = weights * (dweights - jnp.sum(weights * dweights, axis=1, keepdims=True))
    ds2 = two(dscores * HEAD ** (-0.5))
    for i in range(8):
        late_s[i, :, 0:128] = fold(mm(ds2, tperm[i])).astype(BF)
        late_s[i, :, 128:512] = dmexp
    late = group_copies(lambda p: late_s.at[p[0] * 2 + p[3]], late_r, l_ss, l_rs)
    for cp in late:
        cp.start()
    early_r[0] = early_s[m]
    late_r[0] = late_s[m]
    for cp in late:
        cp.wait_recv()

    keys = mm_tl(late_r[:, :, 0:128].reshape(128, 128), early_r[:, :, 128:512].reshape(128, 384))
    vals = mm_tl(early_r[:, :, 0:128].reshape(128, 128), late_r[:, :, 128:512].reshape(128, 384))
    r2_s[:, :, 0:384] = keys.astype(BF).reshape(8, 16, 384)
    r2_s[:, :, 384:768] = vals.astype(BF).reshape(8, 16, 384)
    r2 = []
    for j in NEAR:
        place = at(0, 0, j, 0)
        cp = remote(r2_s.at[place[2]], r2_r.at[j], r2_ss.at[j], r2_rs.at[j], place)
        cp.start()
        r2.append(cp)
    sum2 = r2_s[z].astype(F32)
    for cp, j in zip(r2, NEAR):
        cp.wait_recv()
        sum2 = sum2 + r2_r[j].astype(F32)
    for i in range(2):
        half = sum2[8 * i : 8 * i + 8]
        r3_s[i] = jnp.concatenate([half[:, :384], half[:, 384:]], axis=0).astype(BF)
    r3 = []
    for j in NEAR:
        place = at(0, j, 0, 0)
        src = r3_s.at[lax.rem(place[1], 2)]
        cp = remote(src, r3_r.at[y], r3_ss.at[j], r3_rs.at[j], place)
        cp.start()
        r3.append(cp)
    r3_r[y] = r3_s[yl]
    for cp in r3:
        cp.wait_recv()
    sum3 = r3_r[0].astype(F32)
    for j in range(1, 8):
        sum3 = sum3 + r3_r[j].astype(F32)
    mine = x * 8 + z
    ag_r[mine] = sum3.astype(BF)
    ag = []
    for dx, dz in XZ:
        cp = remote(
            ag_r.at[mine], ag_r.at[mine], ag_ss.at[dx * 8 + dz], ag_rs.at[dx * 8 + dz],
            at(dx, 0, dz, 0),
        )
        cp.start()
        ag.append(cp)
    orow = lax.broadcasted_iota(jnp.int32, (192, 512), 0)
    want = lax.broadcasted_iota(jnp.int32, (192, 512), 1) - ((orow // 6) * 16 + lax.rem(orow, 6))
    for cp in ag:
        cp.wait_recv()
    pieces = ag_r[...].reshape(512, 384)
    grad_out[:, :384] = mm((want == 0).astype(F32).astype(BF), pieces)
    grad_out[:, 384:] = mm((want == 8).astype(F32).astype(BF), pieces)
    for cp in late + r2 + r3 + ag:
        cp.wait_send()


def per_device(tokens, lengths, partner, w_query, w_keyval, w_output):
    vmem = pl.BlockSpec(memory_space=pltpu.VMEM)
    dma = pltpu.SemaphoreType.DMA
    loss, grad = pl.pallas_call(
        kernel,
        name="contrast",
        out_shape=(
            jax.ShapeDtypeStruct((16, 128), F32),
            jax.ShapeDtypeStruct((192, 768), F32),
        ),
        in_specs=[pl.BlockSpec(memory_space=pl.ANY)] * 6,
        out_specs=(vmem, vmem),
        scratch_shapes=[
            pltpu.SMEM((2,), jnp.int32),
            pltpu.SMEM((2,), jnp.int32),
            pltpu.VMEM((640, 768), BF),
            pltpu.VMEM((768, 384), BF),
            pltpu.VMEM((768, 768), BF),
            pltpu.VMEM((384, 768), BF),
            dma((6,)),
            pltpu.VMEM((2, 16, 384), BF),
            pltpu.VMEM((8, 16, 384), BF),
            pltpu.VMEM((8, 8, 16, 768), BF),
            pltpu.VMEM((8, 640, 128), BF),
            pltpu.VMEM((8, 16, 512), BF),
            pltpu.VMEM((8, 16, 512), BF),
            pltpu.VMEM((8, 16, 512), BF),
            pltpu.VMEM((8, 16, 512), BF),
            pltpu.VMEM((8, 16, 768), BF),
            pltpu.VMEM((8, 16, 768), BF),
            pltpu.VMEM((2, 16, 384), BF),
            pltpu.VMEM((8, 16, 384), BF),
            pltpu.VMEM((32, 16, 384), BF),
            pltpu.VMEM((16, 640), F32),
        ]
        + [dma((8,))] * 16
        + [dma((32,))] * 2,
        compiler_params=pltpu.CompilerParams(
            collective_id=0, has_side_effects=True, vmem_limit_bytes=60 * 2**20
        ),
    )(lengths, partner, tokens, w_query, w_keyval, w_output)
    return loss[::8, 0], grad


def solution(mesh):
    in_specs = (P(("col", "rep"), None), P(("col", "rep")), P(("col", "rep")), P(), P(), P())
    out_specs = (P(("col", "rep")), P("rep", None))
    return jax.shard_map(
        per_device, mesh=mesh, in_specs=in_specs, out_specs=out_specs, check_vma=False
    )
```

```python
import functools

import jax
import jax.numpy as jnp
from jax import lax
from jax.experimental import pallas as pl
from jax.experimental.pallas import tpu as pltpu
from jax.sharding import PartitionSpec as P

HEAD = 64
SHARP = 0.07
BF = jnp.bfloat16
F32 = jnp.float32
MESH = pl.DeviceIdType.MESH
NX, NY, NZ = 4, 8, 8
NEAR = (1, 7, 2, 6, 3, 5, 4)

XC = [(dx, dk) for dx in range(NX) for dk in range(2) if (dx, dk) != (0, 0)]
XZ = [(dx, dz) for dx in range(NX) for dz in (0,) + NEAR if (dx, dz) != (0, 0)]
XY = [(dx, dh) for dx in range(NX) for dh in (0, 1, 3, 2) if (dx, dh) != (0, 0)]
PEERS = sorted(
    {(dx, 0, 0, dk) for dx, dk in XC}
    | {(0, j, 0, 0) for j in NEAR}
    | {(0, 0, j, 0) for j in NEAR}
    | {(dx, 0, dz, 0) for dx, dz in XZ}
    | {(dx, 2 * dh, 0, 0) for dx, dh in XY}
)


def mm(a, b):
    return jnp.dot(a, b, preferred_element_type=F32)


def mm_t(a, b):
    return lax.dot_general(a, b, (((1,), (1,)), ((), ())), preferred_element_type=F32)


def mm_tl(a, b):
    return lax.dot_general(a, b, (((0,), (0,)), ((), ())), preferred_element_type=F32)


def two(a):
    high = a.astype(BF)
    low = (a - high.astype(F32)).astype(BF)
    return jnp.concatenate([high, low], axis=0)


def fold(a):
    return a[:16] + a[16:]


def device(x, y, z, k):
    return ((x * NZ + z) * 4 + y // 2, lax.rem(y, 2) * 2 + k)


def kernel(
    lens_h, part_h, tok_h, wq_h, wkv_h, wo_h,
    loss_out, grad_out,
    lens, part, tok, wq, wkv, wo, in_s,
    a1_s, a1_r, u, tperm, early_s, early_r, late_s, late_r, r2k_s, r2k_r, r2v_s, r2v_r,
    r3k_s, r3k_r, r3v_r, agk_r, agv_r,
    soft, a1_ss, a1_rs, a2_ss, a2_rs, a3_ss, a3_rs, fw_ss, fw_rs,
    e_ss, e_rs, l_ss, l_rs, r2k_ss, r2k_rs, r2v_ss, r2v_rs,
    r3k_ss, r3k_rs, r3v_ss, r3v_rs, agv_ss, agv_rs, agk_ss, agk_rs,
):
    col, rep = lax.axis_index("col"), lax.axis_index("rep")
    x, z = col // 32, lax.rem(col // 4, 8)
    yh, yl, k = lax.rem(col, 4), rep // 2, lax.rem(rep, 2)
    y = yh * 2 + yl
    m = x * 2 + k

    def at(dx, dy, dz, dk):
        return (
            lax.rem(x + dx, NX), lax.rem(y + dy, NY), lax.rem(z + dz, NZ), lax.rem(k + dk, 2)
        )

    def remote(src, dst, ss, rs, place):
        return pltpu.make_async_remote_copy(
            src_ref=src, dst_ref=dst, send_sem=ss, recv_sem=rs,
            device_id=device(*place), device_id_type=MESH,
        )

    loads = [
        pltpu.make_async_copy(src, dst, in_s.at[i])
        for i, (src, dst) in enumerate(
            [(lens_h, lens), (tok_h, tok), (wq_h, wq), (wkv_h, wkv), (wo_h, wo), (part_h, part)]
        )
    ]
    for cp in loads:
        cp.start()
    barrier = pltpu.get_barrier_semaphore()
    for off in PEERS:
        pl.semaphore_signal(
            barrier, inc=1, device_id=device(*at(*off)), device_id_type=MESH
        )

    row = lax.broadcasted_iota(jnp.int32, (16, 640), 0)
    pos = lax.broadcasted_iota(jnp.int32, (16, 640), 1)
    loads[0].wait()
    loads[1].wait()
    l0, l1 = lens[0], lens[1]
    lo = jnp.where(row < 8, 0, l0)
    hi = jnp.where(row < 8, l0, l0 + l1)
    t = tok[...]
    first = mm((pos == lo).astype(F32).astype(BF), t)
    hrow = lax.rem(lax.broadcasted_iota(jnp.int32, (16, 384), 0), 8)
    own_head = lax.broadcasted_iota(jnp.int32, (16, 384), 1) // HEAD == hrow
    loads[2].wait()
    query = mm(first.astype(BF), wq[...]).astype(BF).astype(F32)
    qexp = jnp.where(own_head, query, 0.0).astype(BF)
    loads[3].wait()
    wk, wv = wkv[:, :384], wkv[:, 384:]
    scores = fold(mm_t(two(mm_t(qexp, wk)), t)) * HEAD ** (-0.5)
    scores = jnp.where((pos >= lo) & (pos < hi), scores, -1e30)
    lifted = jnp.exp(scores - jnp.max(scores, axis=1, keepdims=True))
    weights = lifted / jnp.sum(lifted, axis=1, keepdims=True)
    soft[...] = weights
    wb = weights.astype(BF)
    pooled = mm(wb, t)
    pooled_b = pooled.astype(BF)
    mixed = jnp.where(own_head, fold(mm(two(pooled), wv)), 0.0)
    mixed = jnp.sum(mixed.reshape(2, 8, 384), axis=1, keepdims=True)
    mixed = jnp.broadcast_to(mixed, (2, 8, 384)).reshape(16, 384).astype(BF)
    loads[4].wait()
    embed = first + mm(mixed, wo[...])
    norm = jnp.sqrt(jnp.sum(embed * embed, axis=1, keepdims=True) + 1e-06)
    unit = embed / norm
    unit_b = unit.astype(BF)
    ub = unit_b.astype(F32)
    row16 = lax.broadcasted_iota(jnp.int32, (16, 768), 0)
    placed = jnp.where(row16 == 2 * m, ub[0:1], jnp.where(row16 == 2 * m + 1, ub[8:9], 0.0))
    placed = placed.astype(BF)
    a1_s[0] = placed[:, :384]
    a1_s[1] = placed[:, 384:]

    pl.semaphore_wait(barrier, len(PEERS))

    def group_copies(src, dst, ss, rs):
        copies = []
        for dx, dk in XC:
            place = at(dx, 0, 0, dk)
            slot = dx * 2 + dk
            copies.append(remote(src(place), dst.at[slot], ss.at[slot], rs.at[slot], place))
        return copies

    a1 = group_copies(lambda p: a1_s.at[p[3]], a1_r, a1_ss, a1_rs)
    for cp in a1:
        cp.start()

    lane = lax.broadcasted_iota(jnp.int32, (768, 128), 1)
    deep = lax.broadcasted_iota(jnp.int32, (768, 128), 0)
    part8, pos16, pos8 = lane // 16, lax.rem(lane, 16), lax.rem(lane, 8)
    by_z = jnp.where(pos8 < 6, (pos16 // 8) * 384 + part8 * 6 + pos8, 100000)
    by_y = jnp.where(pos16 < 12, lax.rem(part8, 2) * 384 + (part8 // 2) * 12 + pos16, 100000)

    def pick(base, i):
        return (deep == base + ((i % 2) * 192 + (i // 2) * 48)).astype(F32).astype(BF)

    def permute(i):
        tperm[i] = mm(tok[...], pick(by_z, i)).astype(BF)

    for cp in a1:
        cp.wait_recv()
    block = a1_s[k].astype(F32)
    for s in range(1, 8):
        block = block + a1_r[s].astype(F32)
    block = block.astype(BF)

    def gather(half):
        lanes = slice(half * 384, half * 384 + 384)
        u[z, y, :, lanes] = block
        mine = u.at[z, y, :, lanes]

        def line(j, second):
            along_z = (half == 0) == second
            return at(0, 0, j, 0) if along_z else at(0, j, 0, 0)

        def plane(j):
            p = at(0, 8 - j, 8 - j, 0)
            return u.at[p[2], :, :, lanes] if half == 0 else u.at[:, p[1], :, lanes]

        own = u.at[z, :, :, lanes] if half == 0 else u.at[:, y, :, lanes]
        a2 = [remote(mine, mine, a2_ss.at[j], a2_rs.at[j], line(j, False)) for j in NEAR]
        for cp in a2:
            cp.start()
        for i in range(3):
            permute(i)
        for cp in a2:
            cp.wait_recv()
        a3 = [remote(own, own, a3_ss.at[j], a3_rs.at[j], line(j, True)) for j in NEAR]
        for cp in a3:
            cp.start()
        fw = []
        for n, j in enumerate((0,) + NEAR):
            if n:
                a3[n - 1].wait_recv()
            reg = own if j == 0 else plane(j)
            cp = remote(reg, reg, fw_ss.at[j], fw_rs.at[j], at(0, 0, 0, 1))
            cp.start()
            fw.append(cp)
            if n == 0:
                for i in range(3, 8):
                    permute(i)
                for i in range(8):
                    early_s[i, :, 0:128] = mm(pooled_b, pick(by_y, i)).astype(BF)
                    early_s[i, :, 128:512] = qexp
                e = group_copies(lambda p: early_s.at[p[0] * 2 + p[3]], early_r, e_ss, e_rs)
                for cp in e:
                    cp.start()
        for cp in fw:
            cp.wait_recv()
        for cp in a2 + a3 + fw:
            cp.wait_send()
        for cp in e:
            cp.wait()

    pl.when(k == 0)(functools.partial(gather, 0))
    pl.when(k == 1)(functools.partial(gather, 1))
    for cp in a1:
        cp.wait_send()

    scale = 1.0 / SHARP
    total = jnp.zeros((1, 1024), F32)
    whole = u[...].reshape(1024, 768)
    for i in range(4):
        part_s = mm_t(u[2 * i : 2 * i + 2].reshape(256, 768), whole)
        total = total + jnp.sum(jnp.exp(part_s * scale), axis=0, keepdims=True)
    all_lse = jnp.log(total)
    logits = mm_t(unit_b, whole) * scale
    lse = jnp.log(jnp.sum(jnp.exp(logits), axis=1, keepdims=True))
    n = lax.broadcasted_iota(jnp.int32, (16, 1024), 1)
    nz, ny, nm, nc = n // 128, lax.rem(n // 16, 8), lax.rem(n // 2, 8), lax.rem(n, 2)
    number = (((nm // 2) * 8 + nz) * 4 + ny // 2) * 4 + lax.rem(ny, 2) * 2 + lax.rem(nm, 2)
    number = number * 2 + nc
    lrow = lax.broadcasted_iota(jnp.int32, (16, 1024), 0)
    loads[5].wait()
    match = number == jnp.where(lrow < 8, part[0], part[1])
    positive = jnp.sum(jnp.where(match, logits, 0.0), axis=1, keepdims=True)
    loss_out[...] = jnp.broadcast_to(lse - positive, (16, 128))
    rowp = jnp.exp(logits - lse).astype(BF)
    colp = jnp.exp(logits - all_lse).astype(BF)
    stack = jnp.concatenate([rowp, colp, match.astype(F32).astype(BF)], axis=0)
    terms = mm(stack, whole)
    dunit = (terms[:16] + terms[16:32] - 2.0 * terms[32:]) / SHARP
    radial = jnp.sum(unit * dunit, axis=1, keepdims=True)
    dembed = (dunit - unit * radial) / norm

    dmixed = fold(mm_t(two(dembed), wo[...])).astype(BF).astype(F32)
    dmexp = jnp.where(own_head, dmixed, 0.0).astype(BF)
    dweights = fold(mm_t(two(mm_t(dmexp, wv)), t)).astype(BF).astype(F32)
    weights = soft[...]
    dscores = weights * (dweights - jnp.sum(weights * dweights, axis=1, keepdims=True))
    ds2 = two(dscores * HEAD ** (-0.5))
    for i in range(8):
        late_s[i, :, 0:128] = fold(mm(ds2, tperm[i])).astype(BF)
        late_s[i, :, 128:512] = dmexp
    late = group_copies(lambda p: late_s.at[p[0] * 2 + p[3]], late_r, l_ss, l_rs)
    for cp in late:
        cp.start()
    early_r[0] = early_s[m]
    late_r[0] = late_s[m]
    for cp in late:
        cp.wait_recv()

    keys = mm_tl(late_r[:, :, 0:128].reshape(128, 128), early_r[:, :, 128:512].reshape(128, 384))
    r2k_s[...] = keys.astype(BF).reshape(8, 16, 384)
    r2k, r2v = [], []
    for j in NEAR:
        place = at(0, 0, j, 0)
        cp = remote(r2k_s.at[place[2]], r2k_r.at[j], r2k_ss.at[j], r2k_rs.at[j], place)
        cp.start()
        r2k.append(cp)
    vals = mm_tl(early_r[:, :, 0:128].reshape(128, 128), late_r[:, :, 128:512].reshape(128, 384))
    r2v_s[...] = vals.astype(BF).reshape(8, 16, 384)
    for j in NEAR:
        place = at(0, j, 0, 0)
        cp = remote(r2v_s.at[place[1]], r2v_r.at[j], r2v_ss.at[j], r2v_rs.at[j], place)
        cp.start()
        r2v.append(cp)

    sum2 = r2k_s[z].astype(F32)
    for cp, j in zip(r2k, NEAR):
        cp.wait_recv()
        sum2 = sum2 + r2k_r[j].astype(F32)
    for i in range(2):
        half = sum2[8 * i : 8 * i + 8]
        tiles = [half[:, :128], half[:, 128:256], half[:, 256:], jnp.zeros((8, 128), F32)]
        r3k_s[i] = jnp.concatenate(tiles, axis=0).astype(BF)
    r3k, r3v = [], []
    for j in NEAR:
        place = at(0, j, 0, 0)
        src = r3k_s.at[lax.rem(place[1], 2)]
        cp = remote(src, r3k_r.at[y], r3k_ss.at[j], r3k_rs.at[j], place)
        cp.start()
        r3k.append(cp)
    r3k_r[y] = r3k_s[yl]
    sum2 = r2v_s[y].astype(F32)
    for cp, j in zip(r2v, NEAR):
        cp.wait_recv()
        sum2 = sum2 + r2v_r[j].astype(F32)
    r3v_r[z] = sum2.astype(BF)
    for j in NEAR:
        cp = remote(r3v_r.at[z], r3v_r.at[z], r3v_ss.at[j], r3v_rs.at[j], at(0, 0, j, 0))
        cp.start()
        r3v.append(cp)

    for cp in r3k:
        cp.wait_recv()
    sum3 = r3k_r[0].astype(F32)
    for j in range(1, 8):
        sum3 = sum3 + r3k_r[j].astype(F32)
    mine = x * 8 + z
    agk_r[mine] = sum3.astype(BF)
    ag = []
    for dx, dz in XZ:
        slot = dx * 8 + dz
        own = agk_r.at[mine]
        cp = remote(own, own, agk_ss.at[slot], agk_rs.at[slot], at(dx, 0, dz, 0))
        cp.start()
        ag.append(cp)
    for cp in r3v:
        cp.wait_recv()
    sum3 = r3v_r[0].astype(F32)
    for j in range(1, 8):
        sum3 = sum3 + r3v_r[j].astype(F32)
    mine_v = x * 4 + yh
    agv_r[mine_v] = sum3.astype(BF)
    for dx, dh in XY:
        slot = dx * 4 + dh
        own = agv_r.at[mine_v]
        cp = remote(own, own, agv_ss.at[slot], agv_rs.at[slot], at(dx, 2 * dh, 0, 0))
        cp.start()
        ag.append(cp)
    krow = lax.broadcasted_iota(jnp.int32, (192, 1024), 0)
    kpos = lax.broadcasted_iota(jnp.int32, (192, 1024), 1)
    kpos = kpos - ((krow // 6) * 32 + lax.rem(krow, 6))
    vrow = lax.broadcasted_iota(jnp.int32, (192, 256), 0)
    vpos = lax.broadcasted_iota(jnp.int32, (192, 256), 1)
    vpos = vpos - ((vrow // 12) * 16 + lax.rem(vrow, 12))
    ksel = [(kpos == 8 * c).astype(F32).astype(BF) for c in range(3)]
    vsel = (vpos == 0).astype(F32).astype(BF)
    for cp in ag:
        cp.wait_recv()
    pieces = agk_r[...].reshape(1024, 128)
    for c in range(3):
        grad_out[:, 128 * c : 128 * c + 128] = mm(ksel[c], pieces)
    grad_out[:, 384:] = mm(vsel, agv_r[...].reshape(256, 384))
    for cp in late + r2k + r2v + r3k + r3v + ag:
        cp.wait_send()


def per_device(tokens, lengths, partner, w_query, w_keyval, w_output):
    vmem = pl.BlockSpec(memory_space=pltpu.VMEM)
    dma = pltpu.SemaphoreType.DMA
    loss, grad = pl.pallas_call(
        kernel,
        name="contrast",
        out_shape=(
            jax.ShapeDtypeStruct((16, 128), F32),
            jax.ShapeDtypeStruct((192, 768), F32),
        ),
        in_specs=[pl.BlockSpec(memory_space=pl.ANY)] * 6,
        out_specs=(vmem, vmem),
        scratch_shapes=[
            pltpu.SMEM((2,), jnp.int32),
            pltpu.SMEM((2,), jnp.int32),
            pltpu.VMEM((640, 768), BF),
            pltpu.VMEM((768, 384), BF),
            pltpu.VMEM((768, 768), BF),
            pltpu.VMEM((384, 768), BF),
            dma((6,)),
            pltpu.VMEM((2, 16, 384), BF),
            pltpu.VMEM((8, 16, 384), BF),
            pltpu.VMEM((8, 8, 16, 768), BF),
            pltpu.VMEM((8, 640, 128), BF),
            pltpu.VMEM((8, 16, 512), BF),
            pltpu.VMEM((8, 16, 512), BF),
            pltpu.VMEM((8, 16, 512), BF),
            pltpu.VMEM((8, 16, 512), BF),
            pltpu.VMEM((8, 16, 384), BF),
            pltpu.VMEM((8, 16, 384), BF),
            pltpu.VMEM((8, 16, 384), BF),
            pltpu.VMEM((8, 16, 384), BF),
            pltpu.VMEM((2, 32, 128), BF),
            pltpu.VMEM((8, 32, 128), BF),
            pltpu.VMEM((8, 16, 384), BF),
            pltpu.VMEM((32, 32, 128), BF),
            pltpu.VMEM((16, 16, 384), BF),
            pltpu.VMEM((16, 640), F32),
        ]
        + [dma((8,))] * 20
        + [dma((16,))] * 2
        + [dma((32,))] * 2,
        compiler_params=pltpu.CompilerParams(
            collective_id=0, has_side_effects=True, vmem_limit_bytes=60 * 2**20
        ),
    )(lengths, partner, tokens, w_query, w_keyval, w_output)
    return loss[::8, 0], grad


def solution(mesh):
    in_specs = (P(("col", "rep"), None), P(("col", "rep")), P(("col", "rep")), P(), P(), P())
    out_specs = (P(("col", "rep")), P("rep", None))
    return jax.shard_map(
        per_device, mesh=mesh, in_specs=in_specs, out_specs=out_specs, check_vma=False
    )
```

```python
import functools

import jax
import jax.numpy as jnp
from jax import lax
from jax.experimental import pallas as pl
from jax.experimental.pallas import tpu as pltpu
from jax.sharding import PartitionSpec as P

HEAD = 64
SHARP = 0.07
BF = jnp.bfloat16
F32 = jnp.float32
MESH = pl.DeviceIdType.MESH
NX, NY, NZ = 4, 8, 8
NEAR = (4, 3, 5, 2, 6, 1, 7)


def hops(offset):
    return -sum(min(d, size - d) for d, size in offset)


XC = sorted(
    [(dx, dk) for dx in range(NX) for dk in range(2) if (dx, dk) != (0, 0)],
    key=lambda o: hops([(o[0], NX)]),
)
XZ = sorted(
    [(dx, dz) for dx in range(NX) for dz in range(NZ) if (dx, dz) != (0, 0)],
    key=lambda o: hops([(o[0], NX), (o[1], NZ)]),
)
XY = sorted(
    [(dx, dh) for dx in range(NX) for dh in range(4) if (dx, dh) != (0, 0)],
    key=lambda o: hops([(o[0], NX), (2 * o[1], NY)]),
)
PEERS = sorted(
    {(dx, 0, 0, dk) for dx, dk in XC}
    | {(0, j, 0, 0) for j in NEAR}
    | {(0, 0, j, 0) for j in NEAR}
    | {(dx, 0, dz, 0) for dx, dz in XZ}
    | {(dx, 2 * dh, 0, 0) for dx, dh in XY}
)


def mm(a, b):
    return jnp.dot(a, b, preferred_element_type=F32)


def mm_t(a, b):
    return lax.dot_general(a, b, (((1,), (1,)), ((), ())), preferred_element_type=F32)


def mm_tl(a, b):
    return lax.dot_general(a, b, (((0,), (0,)), ((), ())), preferred_element_type=F32)


def two(a):
    high = a.astype(BF)
    low = (a - high.astype(F32)).astype(BF)
    return jnp.concatenate([high, low], axis=0)


def fold(a):
    return a[:16] + a[16:]


def device(x, y, z, k):
    return ((x * NZ + z) * 4 + y // 2, lax.rem(y, 2) * 2 + k)


def kernel(
    lens_h, part_h, tok_h, wq_h, wkv_h, wo_h,
    loss_out, grad_out,
    lens, part, tok, wq, wkv, wo, in_s,
    a1_s, a1_r, u, tperm, early_s, early_r, late_s, late_r, r2k_s, r2k_r, r2v_s, r2v_r,
    r3k_s, r3k_r, r3v_r, agk_r, agv_r,
    soft, a1_ss, a1_rs, a2_ss, a2_rs, a3_ss, a3_rs, fw_ss, fw_rs,
    e_ss, e_rs, l_ss, l_rs, r2k_ss, r2k_rs, r2v_ss, r2v_rs,
    r3k_ss, r3k_rs, r3v_ss, r3v_rs, agv_ss, agv_rs, agk_ss, agk_rs,
):
    col, rep = lax.axis_index("col"), lax.axis_index("rep")
    x, z = col // 32, lax.rem(col // 4, 8)
    yh, yl, k = lax.rem(col, 4), rep // 2, lax.rem(rep, 2)
    y = yh * 2 + yl
    m = x * 2 + k

    def at(dx, dy, dz, dk):
        return (
            lax.rem(x + dx, NX), lax.rem(y + dy, NY), lax.rem(z + dz, NZ), lax.rem(k + dk, 2)
        )

    def remote(src, dst, ss, rs, place):
        return pltpu.make_async_remote_copy(
            src_ref=src, dst_ref=dst, send_sem=ss, recv_sem=rs,
            device_id=device(*place), device_id_type=MESH,
        )

    loads = [
        pltpu.make_async_copy(src, dst, in_s.at[i])
        for i, (src, dst) in enumerate(
            [(lens_h, lens), (tok_h, tok), (wq_h, wq), (wkv_h, wkv), (wo_h, wo), (part_h, part)]
        )
    ]
    for cp in loads:
        cp.start()
    barrier = pltpu.get_barrier_semaphore()
    for off in PEERS:
        pl.semaphore_signal(
            barrier, inc=1, device_id=device(*at(*off)), device_id_type=MESH
        )

    row = lax.broadcasted_iota(jnp.int32, (16, 640), 0)
    pos = lax.broadcasted_iota(jnp.int32, (16, 640), 1)
    loads[0].wait()
    loads[1].wait()
    l0, l1 = lens[0], lens[1]
    lo = jnp.where(row < 8, 0, l0)
    hi = jnp.where(row < 8, l0, l0 + l1)
    t = tok[...]
    first = mm((pos == lo).astype(F32).astype(BF), t)
    hrow = lax.rem(lax.broadcasted_iota(jnp.int32, (16, 384), 0), 8)
    own_head = lax.broadcasted_iota(jnp.int32, (16, 384), 1) // HEAD == hrow
    loads[2].wait()
    query = mm(first.astype(BF), wq[...]).astype(BF).astype(F32)
    qexp = jnp.where(own_head, query, 0.0).astype(BF)
    loads[3].wait()
    wk, wv = wkv[:, :384], wkv[:, 384:]
    scores = fold(mm_t(two(mm_t(qexp, wk)), t)) * HEAD ** (-0.5)
    scores = jnp.where((pos >= lo) & (pos < hi), scores, -1e30)
    lifted = jnp.exp(scores - jnp.max(scores, axis=1, keepdims=True))
    weights = lifted / jnp.sum(lifted, axis=1, keepdims=True)
    soft[...] = weights
    wb = weights.astype(BF)
    pooled = mm(wb, t)
    pooled_b = pooled.astype(BF)
    mixed = jnp.where(own_head, fold(mm(two(pooled), wv)), 0.0)
    mixed = jnp.sum(mixed.reshape(2, 8, 384), axis=1, keepdims=True)
    mixed = jnp.broadcast_to(mixed, (2, 8, 384)).reshape(16, 384).astype(BF)
    loads[4].wait()
    embed = first + mm(mixed, wo[...])
    norm = jnp.sqrt(jnp.sum(embed * embed, axis=1, keepdims=True) + 1e-06)
    unit = embed / norm
    unit_b = unit.astype(BF)
    ub = unit_b.astype(F32)
    row16 = lax.broadcasted_iota(jnp.int32, (16, 768), 0)
    placed = jnp.where(row16 == 2 * m, ub[0:1], jnp.where(row16 == 2 * m + 1, ub[8:9], 0.0))
    placed = placed.astype(BF)
    a1_s[0] = placed[:, :384]
    a1_s[1] = placed[:, 384:]

    pl.semaphore_wait(barrier, len(PEERS))

    def group_copies(src, dst, ss, rs):
        copies = []
        for dx, dk in XC:
            place = at(dx, 0, 0, dk)
            slot = dx * 2 + dk
            copies.append(remote(src(place), dst.at[slot], ss.at[slot], rs.at[slot], place))
        return copies

    a1 = group_copies(lambda p: a1_s.at[p[3]], a1_r, a1_ss, a1_rs)
    for cp in a1:
        cp.start()

    lane = lax.broadcasted_iota(jnp.int32, (768, 128), 1)
    deep = lax.broadcasted_iota(jnp.int32, (768, 128), 0)
    part8, pos16, pos8 = lane // 16, lax.rem(lane, 16), lax.rem(lane, 8)
    by_z = jnp.where(pos8 < 6, (pos16 // 8) * 384 + part8 * 6 + pos8, 100000)
    by_y = jnp.where(pos16 < 12, lax.rem(part8, 2) * 384 + (part8 // 2) * 12 + pos16, 100000)

    def pick(base, i):
        return (deep == base + ((i % 2) * 192 + (i // 2) * 48)).astype(F32).astype(BF)

    def permute(i):
        tperm[i] = mm(tok[...], pick(by_z, i)).astype(BF)

    for cp in a1:
        cp.wait_recv()
    block = a1_s[k].astype(F32)
    for s in range(1, 8):
        block = block + a1_r[s].astype(F32)
    block = block.astype(BF)

    def gather(half):
        lanes = slice(half * 384, half * 384 + 384)
        u[z, y, :, lanes] = block
        mine = u.at[z, y, :, lanes]

        def line(j, second):
            along_z = (half == 0) == second
            return at(0, 0, j, 0) if along_z else at(0, j, 0, 0)

        def plane(j):
            p = at(0, 8 - j, 8 - j, 0)
            return u.at[p[2], :, :, lanes] if half == 0 else u.at[:, p[1], :, lanes]

        own = u.at[z, :, :, lanes] if half == 0 else u.at[:, y, :, lanes]
        a2 = [remote(mine, mine, a2_ss.at[j], a2_rs.at[j], line(j, False)) for j in NEAR]
        for cp in a2:
            cp.start()
        for i in range(3):
            permute(i)
        for cp in a2:
            cp.wait_recv()
        a3 = [remote(own, own, a3_ss.at[j], a3_rs.at[j], line(j, True)) for j in NEAR]
        for cp in a3:
            cp.start()
        fw = []
        for n, j in enumerate((0,) + NEAR):
            if n:
                a3[n - 1].wait_recv()
            reg = own if j == 0 else plane(j)
            cp = remote(reg, reg, fw_ss.at[j], fw_rs.at[j], at(0, 0, 0, 1))
            cp.start()
            fw.append(cp)
            if n == 0:
                for i in range(3, 8):
                    permute(i)
                for i in range(8):
                    early_s[i, :, 0:128] = mm(pooled_b, pick(by_y, i)).astype(BF)
                    early_s[i, :, 128:512] = qexp
                e = group_copies(lambda p: early_s.at[p[0] * 2 + p[3]], early_r, e_ss, e_rs)
                for cp in e:
                    cp.start()
        for cp in fw:
            cp.wait_recv()
        for cp in a2 + a3 + fw:
            cp.wait_send()
        for cp in e:
            cp.wait()

    pl.when(k == 0)(functools.partial(gather, 0))
    pl.when(k == 1)(functools.partial(gather, 1))
    for cp in a1:
        cp.wait_send()

    scale = 1.0 / SHARP
    total = jnp.zeros((1, 1024), F32)
    whole = u[...].reshape(1024, 768)
    for i in range(4):
        part_s = mm_t(u[2 * i : 2 * i + 2].reshape(256, 768), whole)
        total = total + jnp.sum(jnp.exp(part_s * scale), axis=0, keepdims=True)
    all_lse = jnp.log(total)
    logits = mm_t(unit_b, whole) * scale
    lse = jnp.log(jnp.sum(jnp.exp(logits), axis=1, keepdims=True))
    n = lax.broadcasted_iota(jnp.int32, (16, 1024), 1)
    nz, ny, nm, nc = n // 128, lax.rem(n // 16, 8), lax.rem(n // 2, 8), lax.rem(n, 2)
    number = (((nm // 2) * 8 + nz) * 4 + ny // 2) * 4 + lax.rem(ny, 2) * 2 + lax.rem(nm, 2)
    number = number * 2 + nc
    lrow = lax.broadcasted_iota(jnp.int32, (16, 1024), 0)
    loads[5].wait()
    match = number == jnp.where(lrow < 8, part[0], part[1])
    positive = jnp.sum(jnp.where(match, logits, 0.0), axis=1, keepdims=True)
    loss = lse - positive
    loss_lane = lax.broadcasted_iota(jnp.int32, (8, 128), 1)
    loss_out[...] = jnp.where(loss_lane == 0, loss[0:8], loss[8:16])
    rowp = jnp.exp(logits - lse).astype(BF)
    colp = jnp.exp(logits - all_lse).astype(BF)
    stack = jnp.concatenate([rowp, colp, match.astype(F32).astype(BF)], axis=0)
    terms = mm(stack, whole)
    dunit = (terms[:16] + terms[16:32] - 2.0 * terms[32:]) / SHARP
    radial = jnp.sum(unit * dunit, axis=1, keepdims=True)
    dembed = (dunit - unit * radial) / norm

    dmixed = fold(mm_t(two(dembed), wo[...])).astype(BF).astype(F32)
    dmexp = jnp.where(own_head, dmixed, 0.0).astype(BF)
    dweights = fold(mm_t(two(mm_t(dmexp, wv)), t)).astype(BF).astype(F32)
    weights = soft[...]
    dscores = weights * (dweights - jnp.sum(weights * dweights, axis=1, keepdims=True))
    ds2 = two(dscores * HEAD ** (-0.5))
    for i in range(8):
        late_s[i, :, 0:128] = fold(mm(ds2, tperm[i])).astype(BF)
        late_s[i, :, 128:512] = dmexp
    late = group_copies(lambda p: late_s.at[p[0] * 2 + p[3]], late_r, l_ss, l_rs)
    for cp in late:
        cp.start()
    early_r[0] = early_s[m]
    late_r[0] = late_s[m]
    for cp in late:
        cp.wait_recv()

    keys = mm_tl(late_r[:, :, 0:128].reshape(128, 128), early_r[:, :, 128:512].reshape(128, 384))
    r2k_s[...] = keys.astype(BF).reshape(8, 16, 384)
    r2k, r2v = [], []
    for j in NEAR:
        place = at(0, 0, j, 0)
        cp = remote(r2k_s.at[place[2]], r2k_r.at[j], r2k_ss.at[j], r2k_rs.at[j], place)
        cp.start()
        r2k.append(cp)
    vals = mm_tl(early_r[:, :, 0:128].reshape(128, 128), late_r[:, :, 128:512].reshape(128, 384))
    r2v_s[...] = vals.astype(BF).reshape(8, 16, 384)
    for j in NEAR:
        place = at(0, j, 0, 0)
        cp = remote(r2v_s.at[place[1]], r2v_r.at[j], r2v_ss.at[j], r2v_rs.at[j], place)
        cp.start()
        r2v.append(cp)

    sum2 = r2k_s[z].astype(F32)
    for cp, j in zip(r2k, NEAR):
        cp.wait_recv()
        sum2 = sum2 + r2k_r[j].astype(F32)
    for i in range(2):
        half = sum2[8 * i : 8 * i + 8]
        tiles = [half[:, :128], half[:, 128:256], half[:, 256:], jnp.zeros((8, 128), F32)]
        r3k_s[i] = jnp.concatenate(tiles, axis=0).astype(BF)
    r3k, r3v = [], []
    for j in NEAR:
        place = at(0, j, 0, 0)
        src = r3k_s.at[lax.rem(place[1], 2)]
        cp = remote(src, r3k_r.at[y], r3k_ss.at[j], r3k_rs.at[j], place)
        cp.start()
        r3k.append(cp)
    r3k_r[y] = r3k_s[yl]
    sum2 = r2v_s[y].astype(F32)
    for cp, j in zip(r2v, NEAR):
        cp.wait_recv()
        sum2 = sum2 + r2v_r[j].astype(F32)
    r3v_r[z] = sum2.astype(BF)
    for j in NEAR:
        cp = remote(r3v_r.at[z], r3v_r.at[z], r3v_ss.at[j], r3v_rs.at[j], at(0, 0, j, 0))
        cp.start()
        r3v.append(cp)

    for cp in r3k:
        cp.wait_recv()
    sum3 = r3k_r[0].astype(F32)
    for j in range(1, 8):
        sum3 = sum3 + r3k_r[j].astype(F32)
    mine = x * 8 + z
    agk_r[mine] = sum3.astype(BF)
    ag = []
    for dx, dz in XZ:
        slot = dx * 8 + dz
        own = agk_r.at[mine]
        cp = remote(own, own, agk_ss.at[slot], agk_rs.at[slot], at(dx, 0, dz, 0))
        cp.start()
        ag.append(cp)
    for cp in r3v:
        cp.wait_recv()
    sum3 = r3v_r[0].astype(F32)
    for j in range(1, 8):
        sum3 = sum3 + r3v_r[j].astype(F32)
    mine_v = x * 4 + yh
    agv_r[mine_v] = sum3.astype(BF)
    for dx, dh in XY:
        slot = dx * 4 + dh
        own = agv_r.at[mine_v]
        cp = remote(own, own, agv_ss.at[slot], agv_rs.at[slot], at(dx, 2 * dh, 0, 0))
        cp.start()
        ag.append(cp)
    krow = lax.broadcasted_iota(jnp.int32, (192, 1024), 0)
    kpos = lax.broadcasted_iota(jnp.int32, (192, 1024), 1)
    kpos = kpos - ((krow // 6) * 32 + lax.rem(krow, 6))
    vrow = lax.broadcasted_iota(jnp.int32, (192, 256), 0)
    vpos = lax.broadcasted_iota(jnp.int32, (192, 256), 1)
    vpos = vpos - ((vrow // 12) * 16 + lax.rem(vrow, 12))
    ksel = [(kpos == 8 * c).astype(F32).astype(BF) for c in range(3)]
    vsel = (vpos == 0).astype(F32).astype(BF)
    for cp in ag:
        cp.wait_recv()
    pieces = agk_r[...].reshape(1024, 128)
    for c in range(3):
        grad_out[:, 128 * c : 128 * c + 128] = mm(ksel[c], pieces).astype(BF)
    grad_out[:, 384:] = mm(vsel, agv_r[...].reshape(256, 384)).astype(BF)
    for cp in late + r2k + r2v + r3k + r3v + ag:
        cp.wait_send()


def per_device(tokens, lengths, partner, w_query, w_keyval, w_output):
    vmem = pl.BlockSpec(memory_space=pltpu.VMEM)
    dma = pltpu.SemaphoreType.DMA
    loss, grad = pl.pallas_call(
        kernel,
        name="contrast",
        out_shape=(
            jax.ShapeDtypeStruct((8, 128), F32),
            jax.ShapeDtypeStruct((192, 768), BF),
        ),
        in_specs=[pl.BlockSpec(memory_space=pl.ANY)] * 6,
        out_specs=(vmem, vmem),
        scratch_shapes=[
            pltpu.SMEM((2,), jnp.int32),
            pltpu.SMEM((2,), jnp.int32),
            pltpu.VMEM((640, 768), BF),
            pltpu.VMEM((768, 384), BF),
            pltpu.VMEM((768, 768), BF),
            pltpu.VMEM((384, 768), BF),
            dma((6,)),
            pltpu.VMEM((2, 16, 384), BF),
            pltpu.VMEM((8, 16, 384), BF),
            pltpu.VMEM((8, 8, 16, 768), BF),
            pltpu.VMEM((8, 640, 128), BF),
            pltpu.VMEM((8, 16, 512), BF),
            pltpu.VMEM((8, 16, 512), BF),
            pltpu.VMEM((8, 16, 512), BF),
            pltpu.VMEM((8, 16, 512), BF),
            pltpu.VMEM((8, 16, 384), BF),
            pltpu.VMEM((8, 16, 384), BF),
            pltpu.VMEM((8, 16, 384), BF),
            pltpu.VMEM((8, 16, 384), BF),
            pltpu.VMEM((2, 32, 128), BF),
            pltpu.VMEM((8, 32, 128), BF),
            pltpu.VMEM((8, 16, 384), BF),
            pltpu.VMEM((32, 32, 128), BF),
            pltpu.VMEM((16, 16, 384), BF),
            pltpu.VMEM((16, 640), F32),
        ]
        + [dma((8,))] * 20
        + [dma((16,))] * 2
        + [dma((32,))] * 2,
        compiler_params=pltpu.CompilerParams(
            collective_id=0, has_side_effects=True, vmem_limit_bytes=60 * 2**20
        ),
    )(lengths, partner, tokens, w_query, w_keyval, w_output)
    return loss[0, :2], grad.astype(F32)


def solution(mesh):
    in_specs = (P(("col", "rep"), None), P(("col", "rep")), P(("col", "rep")), P(), P(), P())
    out_specs = (P(("col", "rep")), P("rep", None))
    return jax.shard_map(
        per_device, mesh=mesh, in_specs=in_specs, out_specs=out_specs, check_vma=False
    )
```

```python
import functools

import jax
import jax.numpy as jnp
from jax import lax
from jax.experimental import pallas as pl
from jax.experimental.pallas import tpu as pltpu
from jax.sharding import PartitionSpec as P

HEAD = 64
SHARP = 0.07
BF = jnp.bfloat16
F32 = jnp.float32
MESH = pl.DeviceIdType.MESH
NX, NY, NZ = 4, 8, 8
NEAR = (4, 3, 5, 2, 6, 1, 7)


def hops(offset):
    return -sum(min(d, size - d) for d, size in offset)


XC = sorted(
    [(dx, dk) for dx in range(NX) for dk in range(2) if (dx, dk) != (0, 0)],
    key=lambda o: hops([(o[0], NX)]),
)
XZ = sorted(
    [(dx, dz) for dx in range(NX) for dz in range(NZ) if (dx, dz) != (0, 0)],
    key=lambda o: hops([(o[0], NX), (o[1], NZ)]),
)
XY = sorted(
    [(dx, dh) for dx in range(NX) for dh in range(4) if (dx, dh) != (0, 0)],
    key=lambda o: hops([(o[0], NX), (2 * o[1], NY)]),
)
PEERS = sorted(
    {(dx, 0, 0, dk) for dx, dk in XC}
    | {(0, j, 0, 0) for j in NEAR}
    | {(0, 0, j, 0) for j in NEAR}
    | {(dx, 0, dz, 0) for dx, dz in XZ}
    | {(dx, 2 * dh, 0, 0) for dx, dh in XY}
)


def mm(a, b):
    return jnp.dot(a, b, preferred_element_type=F32)


def mm_t(a, b):
    return lax.dot_general(a, b, (((1,), (1,)), ((), ())), preferred_element_type=F32)


def mm_tl(a, b):
    return lax.dot_general(a, b, (((0,), (0,)), ((), ())), preferred_element_type=F32)


def two(a):
    high = a.astype(BF)
    low = (a - high.astype(F32)).astype(BF)
    return jnp.concatenate([high, low], axis=0)


def fold(a):
    return a[:16] + a[16:]


def device(x, y, z, k):
    return ((x * NZ + z) * 4 + y // 2, lax.rem(y, 2) * 2 + k)


def kernel(
    meta_h, tok_h, wq_h, wkv_h, wo_h,
    loss_out, grad_out,
    meta, tok, wq, wkv, wo, in_s,
    a1_s, a1_r, u, tperm, early_s, early_r, late_s, late_r, dm_s, dm_r, r2k_s, r2k_r, r2v_s, r2v_r,
    r3k_s, r3k_r, r3v_r, agk_r, agv_r,
    soft, a1_ss, a1_rs, a2_ss, a2_rs, a3_ss, a3_rs, fw_ss, fw_rs,
    e_ss, e_rs, l_ss, l_rs, d_ss, d_rs, r2k_ss, r2k_rs, r2v_ss, r2v_rs,
    r3k_ss, r3k_rs, r3v_ss, r3v_rs, agv_ss, agv_rs, agk_ss, agk_rs,
):
    col, rep = lax.axis_index("col"), lax.axis_index("rep")
    x, z = col // 32, lax.rem(col // 4, 8)
    yh, yl, k = lax.rem(col, 4), rep // 2, lax.rem(rep, 2)
    y = yh * 2 + yl
    m = x * 2 + k

    def at(dx, dy, dz, dk):
        return (
            lax.rem(x + dx, NX), lax.rem(y + dy, NY), lax.rem(z + dz, NZ), lax.rem(k + dk, 2)
        )

    def remote(src, dst, ss, rs, place):
        return pltpu.make_async_remote_copy(
            src_ref=src, dst_ref=dst, send_sem=ss, recv_sem=rs,
            device_id=device(*place), device_id_type=MESH,
        )

    loads = [
        pltpu.make_async_copy(src, dst, in_s.at[i])
        for i, (src, dst) in enumerate(
            [(meta_h, meta), (tok_h, tok), (wq_h, wq), (wkv_h, wkv), (wo_h, wo)]
        )
    ]
    for cp in loads:
        cp.start()
    barrier = pltpu.get_barrier_semaphore()
    for off in PEERS:
        pl.semaphore_signal(
            barrier, inc=1, device_id=device(*at(*off)), device_id_type=MESH
        )

    row = lax.broadcasted_iota(jnp.int32, (16, 640), 0)
    pos = lax.broadcasted_iota(jnp.int32, (16, 640), 1)
    loads[0].wait()
    loads[1].wait()
    l0, l1 = meta[0], meta[1]
    lo = jnp.where(row < 8, 0, l0)
    hi = jnp.where(row < 8, l0, l0 + l1)
    t = tok[...]
    first = mm((pos == lo).astype(F32).astype(BF), t)
    hrow = lax.rem(lax.broadcasted_iota(jnp.int32, (16, 384), 0), 8)
    own_head = lax.broadcasted_iota(jnp.int32, (16, 384), 1) // HEAD == hrow
    loads[2].wait()
    query = mm(first.astype(BF), wq[...]).astype(BF).astype(F32)
    qexp = jnp.where(own_head, query, 0.0).astype(BF)
    loads[3].wait()
    wk, wv = wkv[:, :384], wkv[:, 384:]
    scores = fold(mm_t(two(mm_t(qexp, wk)), t)) * HEAD ** (-0.5)
    scores = jnp.where((pos >= lo) & (pos < hi), scores, -1e30)
    lifted = jnp.exp(scores - jnp.max(scores, axis=1, keepdims=True))
    weights = lifted / jnp.sum(lifted, axis=1, keepdims=True)
    soft[...] = weights
    wb = weights.astype(BF)
    pooled = mm(wb, t)
    pooled_b = pooled.astype(BF)
    mixed = jnp.where(own_head, fold(mm(two(pooled), wv)), 0.0)
    mixed = jnp.sum(mixed.reshape(2, 8, 384), axis=1, keepdims=True)
    mixed = jnp.broadcast_to(mixed, (2, 8, 384)).reshape(16, 384).astype(BF)
    loads[4].wait()
    embed = first + mm(mixed, wo[...])
    norm = jnp.sqrt(jnp.sum(embed * embed, axis=1, keepdims=True) + 1e-06)
    unit = embed / norm
    unit_b = unit.astype(BF)
    ub = unit_b.astype(F32)
    row16 = lax.broadcasted_iota(jnp.int32, (16, 768), 0)
    placed = jnp.where(row16 == 2 * m, ub[0:1], jnp.where(row16 == 2 * m + 1, ub[8:9], 0.0))
    placed = placed.astype(BF)
    a1_s[0] = placed[:, :384]
    a1_s[1] = placed[:, 384:]

    pl.semaphore_wait(barrier, len(PEERS))

    def group_copies(src, dst, ss, rs):
        copies = []
        for dx, dk in XC:
            place = at(dx, 0, 0, dk)
            slot = dx * 2 + dk
            copies.append(remote(src(place), dst.at[slot], ss.at[slot], rs.at[slot], place))
        return copies

    a1 = group_copies(lambda p: a1_s.at[p[3]], a1_r, a1_ss, a1_rs)
    for cp in a1:
        cp.start()

    lane = lax.broadcasted_iota(jnp.int32, (768, 128), 1)
    deep = lax.broadcasted_iota(jnp.int32, (768, 128), 0)
    part8, pos16, pos8 = lane // 16, lax.rem(lane, 16), lax.rem(lane, 8)
    by_z = jnp.where(pos8 < 6, (pos16 // 8) * 384 + part8 * 6 + pos8, 100000)
    by_y = jnp.where(pos16 < 12, lax.rem(part8, 2) * 384 + (part8 // 2) * 12 + pos16, 100000)

    def pick(base, i):
        return (deep == base + ((i % 2) * 192 + (i // 2) * 48)).astype(F32).astype(BF)

    def permute(i):
        tperm[i] = mm(tok[...], pick(by_z, i)).astype(BF)

    for i in range(2):
        permute(i)
    for cp in a1:
        cp.wait_recv()
    block = a1_s[k].astype(F32)
    for s in range(1, 8):
        block = block + a1_r[s].astype(F32)
    block = block.astype(BF)

    def gather(half):
        lanes = slice(half * 384, half * 384 + 384)
        u[z, y, :, lanes] = block
        mine = u.at[z, y, :, lanes]

        def line(j, second):
            along_z = (half == 0) == second
            return at(0, 0, j, 0) if along_z else at(0, j, 0, 0)

        def plane(j):
            p = at(0, 8 - j, 8 - j, 0)
            return u.at[p[2], :, :, lanes] if half == 0 else u.at[:, p[1], :, lanes]

        own = u.at[z, :, :, lanes] if half == 0 else u.at[:, y, :, lanes]
        a2 = {j: remote(mine, mine, a2_ss.at[j], a2_rs.at[j], line(j, False)) for j in NEAR}
        for j in NEAR:
            a2[j].start()

        def spread(j):
            p = at(0, 8 - j, 8 - j, 0)
            part = u.at[z, p[1], :, lanes] if half == 0 else u.at[p[2], y, :, lanes]
            for d in NEAR:
                remote(part, part, a3_ss.at[d], a3_rs.at[d], line(d, True)).start()

        spread(8)
        for j in reversed(NEAR):
            a2[j].wait_recv()
            spread(j)
        a3 = [remote(own, own, a3_ss.at[j], a3_rs.at[j], line(j, True)) for j in NEAR]
        fw = []
        for n, j in enumerate((0,) + NEAR):
            if n:
                a3[n - 1].wait_recv()
            reg = own if j == 0 else plane(j)
            cp = remote(reg, reg, fw_ss.at[j], fw_rs.at[j], at(0, 0, 0, 1))
            cp.start()
            fw.append(cp)
            if n == 0:
                for i in range(2, 8):
                    permute(i)
                for i in range(8):
                    early_s[i, :, 0:128] = mm(pooled_b, pick(by_y, i)).astype(BF)
                    early_s[i, :, 128:512] = qexp
                e = group_copies(lambda p: early_s.at[p[0] * 2 + p[3]], early_r, e_ss, e_rs)
                for cp in e:
                    cp.start()
        for cp in fw:
            cp.wait_recv()
        for cp in list(a2.values()) + a3 + fw:
            cp.wait_send()
        for cp in e:
            cp.wait()

    pl.when(k == 0)(functools.partial(gather, 0))
    pl.when(k == 1)(functools.partial(gather, 1))
    for cp in a1:
        cp.wait_send()

    scale = 1.0 / SHARP
    total = jnp.zeros((1, 1024), F32)
    whole = u[...].reshape(1024, 768)
    for i in range(4):
        part_s = mm_t(u[2 * i : 2 * i + 2].reshape(256, 768), whole)
        total = total + jnp.sum(jnp.exp(part_s * scale), axis=0, keepdims=True)
    all_lse = jnp.log(total)
    logits = mm_t(unit_b, whole) * scale
    lse = jnp.log(jnp.sum(jnp.exp(logits), axis=1, keepdims=True))
    n = lax.broadcasted_iota(jnp.int32, (16, 1024), 1)
    nz, ny, nm, nc = n // 128, lax.rem(n // 16, 8), lax.rem(n // 2, 8), lax.rem(n, 2)
    number = (((nm // 2) * 8 + nz) * 4 + ny // 2) * 4 + lax.rem(ny, 2) * 2 + lax.rem(nm, 2)
    number = number * 2 + nc
    lrow = lax.broadcasted_iota(jnp.int32, (16, 1024), 0)
    match = number == jnp.where(lrow < 8, meta[2], meta[3])
    positive = jnp.sum(jnp.where(match, logits, 0.0), axis=1, keepdims=True)
    loss = lse - positive
    loss_lane = lax.broadcasted_iota(jnp.int32, (8, 128), 1)
    loss_out[...] = jnp.where(loss_lane == 0, loss[0:8], loss[8:16])
    rowp = jnp.exp(logits - lse).astype(BF)
    colp = jnp.exp(logits - all_lse).astype(BF)
    stack = jnp.concatenate([rowp, colp, match.astype(F32).astype(BF)], axis=0)
    terms = mm(stack, whole)
    dunit = (terms[:16] + terms[16:32] - 2.0 * terms[32:]) / SHARP
    radial = jnp.sum(unit * dunit, axis=1, keepdims=True)
    dembed = (dunit - unit * radial) / norm

    dmixed = fold(mm_t(two(dembed), wo[...])).astype(BF).astype(F32)
    dmexp = jnp.where(own_head, dmixed, 0.0).astype(BF)
    dm_s[...] = dmexp
    dm = group_copies(lambda p: dm_s, dm_r, d_ss, d_rs)
    for cp in dm:
        cp.start()
    dm_r[0] = dmexp
    dweights = fold(mm_t(two(mm_t(dmexp, wv)), t)).astype(BF).astype(F32)
    weights = soft[...]
    dscores = weights * (dweights - jnp.sum(weights * dweights, axis=1, keepdims=True))
    ds2 = two(dscores * HEAD ** (-0.5))
    for i in range(8):
        late_s[i] = fold(mm(ds2, tperm[i])).astype(BF)
    late = group_copies(lambda p: late_s.at[p[0] * 2 + p[3]], late_r, l_ss, l_rs)
    for cp in late:
        cp.start()
    early_r[0] = early_s[m]
    late_r[0] = late_s[m]

    r2k, r2v = [], []
    for cp in dm:
        cp.wait_recv()
    vals = mm_tl(early_r[:, :, 0:128].reshape(128, 128), dm_r[...].reshape(128, 384))
    r2v_s[...] = vals.astype(BF).reshape(8, 16, 384)
    for j in NEAR:
        place = at(0, j, 0, 0)
        cp = remote(r2v_s.at[place[1]], r2v_r.at[j], r2v_ss.at[j], r2v_rs.at[j], place)
        cp.start()
        r2v.append(cp)
    for cp in late:
        cp.wait_recv()
    keys = mm_tl(late_r[...].reshape(128, 128), early_r[:, :, 128:512].reshape(128, 384))
    r2k_s[...] = keys.astype(BF).reshape(8, 16, 384)
    for j in NEAR:
        place = at(0, 0, j, 0)
        cp = remote(r2k_s.at[place[2]], r2k_r.at[j], r2k_ss.at[j], r2k_rs.at[j], place)
        cp.start()
        r2k.append(cp)
    sum2 = r2k_s[z].astype(F32)
    for cp, j in zip(r2k, NEAR):
        cp.wait_recv()
        sum2 = sum2 + r2k_r[j].astype(F32)
    for i in range(2):
        half = sum2[8 * i : 8 * i + 8]
        tiles = [half[:, :128], half[:, 128:256], half[:, 256:], jnp.zeros((8, 128), F32)]
        r3k_s[i] = jnp.concatenate(tiles, axis=0).astype(BF)
    r3k, r3v = [], []
    for j in NEAR:
        place = at(0, j, 0, 0)
        src = r3k_s.at[lax.rem(place[1], 2)]
        cp = remote(src, r3k_r.at[y], r3k_ss.at[j], r3k_rs.at[j], place)
        cp.start()
        r3k.append(cp)
    r3k_r[y] = r3k_s[yl]
    sum2 = r2v_s[y].astype(F32)
    for cp, j in zip(r2v, NEAR):
        cp.wait_recv()
        sum2 = sum2 + r2v_r[j].astype(F32)
    r3v_r[z] = sum2.astype(BF)
    for j in NEAR:
        cp = remote(r3v_r.at[z], r3v_r.at[z], r3v_ss.at[j], r3v_rs.at[j], at(0, 0, j, 0))
        cp.start()
        r3v.append(cp)

    for cp in r3k:
        cp.wait_recv()
    sum3 = r3k_r[0].astype(F32)
    for j in range(1, 8):
        sum3 = sum3 + r3k_r[j].astype(F32)
    mine = x * 8 + z
    agk_r[mine] = sum3.astype(BF)
    ag = []
    for dx, dz in XZ:
        slot = dx * 8 + dz
        own = agk_r.at[mine]
        cp = remote(own, own, agk_ss.at[slot], agk_rs.at[slot], at(dx, 0, dz, 0))
        cp.start()
        ag.append(cp)
    for cp in r3v:
        cp.wait_recv()
    sum3 = r3v_r[0].astype(F32)
    for j in range(1, 8):
        sum3 = sum3 + r3v_r[j].astype(F32)
    mine_v = x * 4 + yh
    agv_r[mine_v] = sum3.astype(BF)
    for dx, dh in XY:
        slot = dx * 4 + dh
        own = agv_r.at[mine_v]
        cp = remote(own, own, agv_ss.at[slot], agv_rs.at[slot], at(dx, 2 * dh, 0, 0))
        cp.start()
        ag.append(cp)
    krow = lax.broadcasted_iota(jnp.int32, (192, 1024), 0)
    kpos = lax.broadcasted_iota(jnp.int32, (192, 1024), 1)
    kpos = kpos - ((krow // 6) * 32 + lax.rem(krow, 6))
    vrow = lax.broadcasted_iota(jnp.int32, (192, 256), 0)
    vpos = lax.broadcasted_iota(jnp.int32, (192, 256), 1)
    vpos = vpos - ((vrow // 12) * 16 + lax.rem(vrow, 12))
    ksel = [(kpos == 8 * c).astype(F32).astype(BF) for c in range(3)]
    vsel = (vpos == 0).astype(F32).astype(BF)
    for cp in ag:
        cp.wait_recv()
    pieces = agk_r[...].reshape(1024, 128)
    for c in range(3):
        grad_out[:, 128 * c : 128 * c + 128] = mm(ksel[c], pieces).astype(BF)
    grad_out[:, 384:] = mm(vsel, agv_r[...].reshape(256, 384)).astype(BF)
    for cp in dm + late + r2k + r2v + r3k + r3v + ag:
        cp.wait_send()


def per_device(tokens, lengths, partner, w_query, w_keyval, w_output):
    vmem = pl.BlockSpec(memory_space=pltpu.VMEM)
    dma = pltpu.SemaphoreType.DMA
    loss, grad = pl.pallas_call(
        kernel,
        name="contrast",
        out_shape=(
            jax.ShapeDtypeStruct((8, 128), F32),
            jax.ShapeDtypeStruct((192, 768), BF),
        ),
        in_specs=[pl.BlockSpec(memory_space=pl.ANY)] * 5,
        out_specs=(vmem, vmem),
        scratch_shapes=[
            pltpu.SMEM((4,), jnp.int32),
            pltpu.VMEM((640, 768), BF),
            pltpu.VMEM((768, 384), BF),
            pltpu.VMEM((768, 768), BF),
            pltpu.VMEM((384, 768), BF),
            dma((5,)),
            pltpu.VMEM((2, 16, 384), BF),
            pltpu.VMEM((8, 16, 384), BF),
            pltpu.VMEM((8, 8, 16, 768), BF),
            pltpu.VMEM((8, 640, 128), BF),
            pltpu.VMEM((8, 16, 512), BF),
            pltpu.VMEM((8, 16, 512), BF),
            pltpu.VMEM((8, 16, 128), BF),
            pltpu.VMEM((8, 16, 128), BF),
            pltpu.VMEM((16, 384), BF),
            pltpu.VMEM((8, 16, 384), BF),
            pltpu.VMEM((8, 16, 384), BF),
            pltpu.VMEM((8, 16, 384), BF),
            pltpu.VMEM((8, 16, 384), BF),
            pltpu.VMEM((8, 16, 384), BF),
            pltpu.VMEM((2, 32, 128), BF),
            pltpu.VMEM((8, 32, 128), BF),
            pltpu.VMEM((8, 16, 384), BF),
            pltpu.VMEM((32, 32, 128), BF),
            pltpu.VMEM((16, 16, 384), BF),
            pltpu.VMEM((16, 640), F32),
        ]
        + [dma((8,))] * 22
        + [dma((16,))] * 2
        + [dma((32,))] * 2,
        compiler_params=pltpu.CompilerParams(
            collective_id=0, has_side_effects=True, vmem_limit_bytes=107 * 2**19
        ),
    )(jnp.concatenate([lengths, partner]), tokens, w_query, w_keyval, w_output)
    return loss[0, :2], grad.astype(F32)


def solution(mesh):
    in_specs = (P(("col", "rep"), None), P(("col", "rep")), P(("col", "rep")), P(), P(), P())
    out_specs = (P(("col", "rep")), P("rep", None))
    return jax.shard_map(
        per_device, mesh=mesh, in_specs=in_specs, out_specs=out_specs, check_vma=False
    )
```

```python
import functools

import jax
import jax.numpy as jnp
from jax import lax
from jax.experimental import pallas as pl
from jax.experimental.pallas import tpu as pltpu
from jax.sharding import PartitionSpec as P

HEAD = 64
SHARP = 0.07
BF = jnp.bfloat16
F32 = jnp.float32
MESH = pl.DeviceIdType.MESH
NX, NY, NZ = 4, 8, 8
NEAR = (4, 3, 5, 2, 6, 1, 7)


def hops(offset):
    return -sum(min(d, size - d) for d, size in offset)


XC = sorted(
    [(dx, dk) for dx in range(NX) for dk in range(2) if (dx, dk) != (0, 0)],
    key=lambda o: hops([(o[0], NX)]),
)
XZ = sorted(
    [(dx, dz) for dx in range(NX) for dz in range(NZ) if (dx, dz) != (0, 0)],
    key=lambda o: hops([(o[0], NX), (o[1], NZ)]),
)
XY = sorted(
    [(dx, dh) for dx in range(NX) for dh in range(4) if (dx, dh) != (0, 0)],
    key=lambda o: hops([(o[0], NX), (2 * o[1], NY)]),
)
PEERS = sorted(
    {(dx, 0, 0, dk) for dx, dk in XC}
    | {(0, j, 0, 0) for j in NEAR}
    | {(0, 0, j, 0) for j in NEAR}
    | {(dx, 0, dz, 0) for dx, dz in XZ}
    | {(dx, 2 * dh, 0, 0) for dx, dh in XY}
)


def mm(a, b):
    return jnp.dot(a, b, preferred_element_type=F32)


def mm_t(a, b):
    return lax.dot_general(a, b, (((1,), (1,)), ((), ())), preferred_element_type=F32)


def mm_tl(a, b):
    return lax.dot_general(a, b, (((0,), (0,)), ((), ())), preferred_element_type=F32)


def two(a):
    high = a.astype(BF)
    low = (a - high.astype(F32)).astype(BF)
    return jnp.concatenate([high, low], axis=0)


def fold(a):
    return a[:16] + a[16:]


def device(x, y, z, k):
    return ((x * NZ + z) * 4 + y // 2, lax.rem(y, 2) * 2 + k)


def kernel(
    meta_h, tok_h, wq_h, wkv_h, wo_h,
    loss_out, grad_out,
    meta, tok, wq, wkv, wo, in_s,
    a1_s, a1_r, u, tperm, early_s, early_r, late_s, late_r, dm_s, dm_r, r2k_s, r2k_r, r2v_s, r2v_r,
    r3k_s, r3k_r, r3v_r, agk_r, agv_r,
    soft, a1_ss, a1_rs, a2_ss, a2_rs, a3_ss, a3_rs, fw_ss, fw_rs,
    e_ss, e_rs, l_ss, l_rs, d_ss, d_rs, r2k_ss, r2k_rs, r2v_ss, r2v_rs,
    r3k_ss, r3k_rs, r3v_ss, r3v_rs, agv_ss, agv_rs, agk_ss, agk_rs,
):
    col, rep = lax.axis_index("col"), lax.axis_index("rep")
    x, z = col // 32, lax.rem(col // 4, 8)
    yh, yl, k = lax.rem(col, 4), rep // 2, lax.rem(rep, 2)
    y = yh * 2 + yl
    m = x * 2 + k

    def at(dx, dy, dz, dk):
        return (
            lax.rem(x + dx, NX), lax.rem(y + dy, NY), lax.rem(z + dz, NZ), lax.rem(k + dk, 2)
        )

    def remote(src, dst, ss, rs, place):
        return pltpu.make_async_remote_copy(
            src_ref=src, dst_ref=dst, send_sem=ss, recv_sem=rs,
            device_id=device(*place), device_id_type=MESH,
        )

    loads = [
        pltpu.make_async_copy(src, dst, in_s.at[i])
        for i, (src, dst) in enumerate(
            [(meta_h, meta), (tok_h, tok), (wq_h, wq), (wkv_h, wkv), (wo_h, wo)]
        )
    ]
    for cp in loads:
        cp.start()
    barrier = pltpu.get_barrier_semaphore()
    for off in PEERS:
        pl.semaphore_signal(
            barrier, inc=1, device_id=device(*at(*off)), device_id_type=MESH
        )

    row = lax.broadcasted_iota(jnp.int32, (16, 640), 0)
    pos = lax.broadcasted_iota(jnp.int32, (16, 640), 1)
    loads[0].wait()
    loads[1].wait()
    l0, l1 = meta[0], meta[1]
    lo = jnp.where(row < 8, 0, l0)
    hi = jnp.where(row < 8, l0, l0 + l1)
    t = tok[...]
    first = mm((pos == lo).astype(F32).astype(BF), t)
    hrow = lax.rem(lax.broadcasted_iota(jnp.int32, (16, 384), 0), 8)
    own_head = lax.broadcasted_iota(jnp.int32, (16, 384), 1) // HEAD == hrow
    loads[2].wait()
    query = mm(first.astype(BF), wq[...]).astype(BF).astype(F32)
    qexp = jnp.where(own_head, query, 0.0).astype(BF)
    loads[3].wait()
    wk, wv = wkv[:, :384], wkv[:, 384:]
    scores = fold(mm_t(two(mm_t(qexp, wk)), t)) * HEAD ** (-0.5)
    scores = jnp.where((pos >= lo) & (pos < hi), scores, -1e30)
    lifted = jnp.exp(scores - jnp.max(scores, axis=1, keepdims=True))
    weights = lifted / jnp.sum(lifted, axis=1, keepdims=True)
    soft[...] = weights
    wb = weights.astype(BF)
    pooled = mm(wb, t)
    pooled_b = pooled.astype(BF)
    mixed = jnp.where(own_head, fold(mm(two(pooled), wv)), 0.0)
    mixed = jnp.sum(mixed.reshape(2, 8, 384), axis=1, keepdims=True)
    mixed = jnp.broadcast_to(mixed, (2, 8, 384)).reshape(16, 384).astype(BF)
    loads[4].wait()
    embed = first + mm(mixed, wo[...])
    norm = jnp.sqrt(jnp.sum(embed * embed, axis=1, keepdims=True) + 1e-06)
    unit = embed / norm
    unit_b = unit.astype(BF)
    ub = unit_b.astype(F32)
    row16 = lax.broadcasted_iota(jnp.int32, (16, 768), 0)
    placed = jnp.where(row16 == 2 * m, ub[0:1], jnp.where(row16 == 2 * m + 1, ub[8:9], 0.0))
    placed = placed.astype(BF)
    a1_s[0] = placed[:, :384]
    a1_s[1] = placed[:, 384:]

    pl.semaphore_wait(barrier, len(PEERS))

    def group_copies(src, dst, ss, rs):
        copies = []
        for dx, dk in XC:
            place = at(dx, 0, 0, dk)
            slot = dx * 2 + dk
            copies.append(remote(src(place), dst.at[slot], ss.at[slot], rs.at[slot], place))
        return copies

    a1 = group_copies(lambda p: a1_s.at[p[3]], a1_r, a1_ss, a1_rs)
    for cp in a1:
        cp.start()

    lane = lax.broadcasted_iota(jnp.int32, (768, 128), 1)
    deep = lax.broadcasted_iota(jnp.int32, (768, 128), 0)
    part8, pos16, pos8 = lane // 16, lax.rem(lane, 16), lax.rem(lane, 8)
    by_z = jnp.where(pos8 < 6, (pos16 // 8) * 384 + part8 * 6 + pos8, 100000)
    by_y = jnp.where(pos16 < 12, lax.rem(part8, 2) * 384 + (part8 // 2) * 12 + pos16, 100000)

    def pick(base, i):
        return (deep == base + ((i % 2) * 192 + (i // 2) * 48)).astype(F32).astype(BF)

    def permute(i):
        tperm[i] = mm(tok[...], pick(by_z, i)).astype(BF)

    for i in range(2):
        permute(i)
    for cp in a1:
        cp.wait_recv()
    block = a1_s[k].astype(F32)
    for s in range(1, 8):
        block = block + a1_r[s].astype(F32)
    block = block.astype(BF)

    def gather(half):
        lanes = slice(half * 384, half * 384 + 384)
        u[z, y, :, lanes] = block
        mine = u.at[z, y, :, lanes]

        def line(j, second):
            along_z = (half == 0) == second
            return at(0, 0, j, 0) if along_z else at(0, j, 0, 0)

        def plane(j):
            p = at(0, 8 - j, 8 - j, 0)
            return u.at[p[2], :, :, lanes] if half == 0 else u.at[:, p[1], :, lanes]

        own = u.at[z, :, :, lanes] if half == 0 else u.at[:, y, :, lanes]
        a2 = {j: remote(mine, mine, a2_ss.at[j], a2_rs.at[j], line(j, False)) for j in NEAR}
        for j in NEAR:
            a2[j].start()

        def spread(j):
            p = at(0, 8 - j, 8 - j, 0)
            part = u.at[z, p[1], :, lanes] if half == 0 else u.at[p[2], y, :, lanes]
            for d in NEAR:
                remote(part, part, a3_ss.at[d], a3_rs.at[d], line(d, True)).start()

        spread(8)
        for j in reversed(NEAR):
            a2[j].wait_recv()
            spread(j)
        near = NEAR[::-1]
        a3 = [remote(own, own, a3_ss.at[j], a3_rs.at[j], line(j, True)) for j in near]
        fw = []
        for n, j in enumerate((0,) + near):
            if n:
                a3[n - 1].wait_recv()
            reg = own if j == 0 else plane(j)
            cp = remote(reg, reg, fw_ss.at[j], fw_rs.at[j], at(0, 0, 0, 1))
            cp.start()
            fw.append(cp)
            if n == 0:
                for i in range(2, 8):
                    permute(i)
                for i in range(8):
                    early_s[i, :, 0:128] = mm(pooled_b, pick(by_y, i)).astype(BF)
                    early_s[i, :, 128:512] = qexp
                e = group_copies(lambda p: early_s.at[p[0] * 2 + p[3]], early_r, e_ss, e_rs)
                for cp in e:
                    cp.start()
        for cp in fw:
            cp.wait_recv()
        for cp in list(a2.values()) + a3 + fw:
            cp.wait_send()
        for cp in e:
            cp.wait()

    pl.when(k == 0)(functools.partial(gather, 0))
    pl.when(k == 1)(functools.partial(gather, 1))
    for cp in a1:
        cp.wait_send()

    scale = 1.0 / SHARP
    whole = u[...].reshape(1024, 768)
    totals = [jnp.zeros((1, 256), F32)] * 4
    for i in range(4):
        rows = u[2 * i : 2 * i + 2].reshape(256, 768)
        if i == 0:
            rows = jnp.concatenate([rows, unit_b], axis=0)
        block_s = mm_t(rows, u[2 * i :].reshape(1024 - 256 * i, 768)) * scale
        if i == 0:
            logits, block_s = block_s[256:], block_s[:256]
        expd = jnp.exp(block_s)
        down = jnp.sum(expd, axis=0, keepdims=True)
        for j in range(i, 4):
            totals[j] = totals[j] + down[:, 256 * (j - i) : 256 * (j - i) + 256]
        if i < 3:
            ones = jnp.ones((16, 768 - 256 * i), BF)
            totals[i] = totals[i] + mm_t(ones, expd[:, 256:].astype(BF))[0:1]
    all_lse = jnp.log(jnp.concatenate(totals, axis=1))
    lse = jnp.log(jnp.sum(jnp.exp(logits), axis=1, keepdims=True))
    n = lax.broadcasted_iota(jnp.int32, (16, 1024), 1)
    nz, ny, nm, nc = n // 128, lax.rem(n // 16, 8), lax.rem(n // 2, 8), lax.rem(n, 2)
    number = (((nm // 2) * 8 + nz) * 4 + ny // 2) * 4 + lax.rem(ny, 2) * 2 + lax.rem(nm, 2)
    number = number * 2 + nc
    lrow = lax.broadcasted_iota(jnp.int32, (16, 1024), 0)
    match = number == jnp.where(lrow < 8, meta[2], meta[3])
    positive = jnp.sum(jnp.where(match, logits, 0.0), axis=1, keepdims=True)
    loss = lse - positive
    loss_lane = lax.broadcasted_iota(jnp.int32, (8, 128), 1)
    loss_out[...] = jnp.where(loss_lane == 0, loss[0:8], loss[8:16])
    rowp = jnp.exp(logits - lse).astype(BF)
    colp = jnp.exp(logits - all_lse).astype(BF)
    stack = jnp.concatenate([rowp, colp, match.astype(F32).astype(BF)], axis=0)
    terms = mm(stack, whole)
    dunit = (terms[:16] + terms[16:32] - 2.0 * terms[32:]) / SHARP
    radial = jnp.sum(unit * dunit, axis=1, keepdims=True)
    dembed = (dunit - unit * radial) / norm

    dmixed = fold(mm_t(two(dembed), wo[...])).astype(BF).astype(F32)
    dmexp = jnp.where(own_head, dmixed, 0.0).astype(BF)
    dm_s[...] = dmexp
    dm = group_copies(lambda p: dm_s, dm_r, d_ss, d_rs)
    for cp in dm:
        cp.start()
    dm_r[0] = dmexp
    dweights = fold(mm_t(two(mm_t(dmexp, wv)), t)).astype(BF).astype(F32)
    weights = soft[...]
    dscores = weights * (dweights - jnp.sum(weights * dweights, axis=1, keepdims=True))
    ds2 = two(dscores * HEAD ** (-0.5))
    for i in range(8):
        late_s[i] = fold(mm(ds2, tperm[i])).astype(BF)
    late = group_copies(lambda p: late_s.at[p[0] * 2 + p[3]], late_r, l_ss, l_rs)
    for cp in late:
        cp.start()
    early_r[0] = early_s[m]
    late_r[0] = late_s[m]

    r2k, r2v = [], []
    for cp in dm:
        cp.wait_recv()
    vals = mm_tl(early_r[:, :, 0:128].reshape(128, 128), dm_r[...].reshape(128, 384))
    r2v_s[...] = vals.astype(BF).reshape(8, 16, 384)
    for j in NEAR:
        place = at(0, j, 0, 0)
        cp = remote(r2v_s.at[place[1]], r2v_r.at[j], r2v_ss.at[j], r2v_rs.at[j], place)
        cp.start()
        r2v.append(cp)
    for cp in late:
        cp.wait_recv()
    keys = mm_tl(late_r[...].reshape(128, 128), early_r[:, :, 128:512].reshape(128, 384))
    r2k_s[...] = keys.astype(BF).reshape(8, 16, 384)
    for j in NEAR:
        place = at(0, 0, j, 0)
        cp = remote(r2k_s.at[place[2]], r2k_r.at[j], r2k_ss.at[j], r2k_rs.at[j], place)
        cp.start()
        r2k.append(cp)
    sum2 = r2k_s[z].astype(F32)
    for cp, j in zip(r2k, NEAR):
        cp.wait_recv()
        sum2 = sum2 + r2k_r[j].astype(F32)
    for i in range(2):
        half = sum2[8 * i : 8 * i + 8]
        tiles = [half[:, :128], half[:, 128:256], half[:, 256:], jnp.zeros((8, 128), F32)]
        r3k_s[i] = jnp.concatenate(tiles, axis=0).astype(BF)
    r3k, r3v = [], []
    for j in NEAR:
        place = at(0, j, 0, 0)
        src = r3k_s.at[lax.rem(place[1], 2)]
        cp = remote(src, r3k_r.at[y], r3k_ss.at[j], r3k_rs.at[j], place)
        cp.start()
        r3k.append(cp)
    r3k_r[y] = r3k_s[yl]
    sum2 = r2v_s[y].astype(F32)
    for cp, j in zip(r2v, NEAR):
        cp.wait_recv()
        sum2 = sum2 + r2v_r[j].astype(F32)
    r3v_r[z] = sum2.astype(BF)
    for j in NEAR:
        cp = remote(r3v_r.at[z], r3v_r.at[z], r3v_ss.at[j], r3v_rs.at[j], at(0, 0, j, 0))
        cp.start()
        r3v.append(cp)

    for cp in r3k:
        cp.wait_recv()
    sum3 = r3k_r[0].astype(F32)
    for j in range(1, 8):
        sum3 = sum3 + r3k_r[j].astype(F32)
    mine = x * 8 + z
    agk_r[mine] = sum3.astype(BF)
    ag = []
    for dx, dz in XZ:
        slot = dx * 8 + dz
        own = agk_r.at[mine]
        cp = remote(own, own, agk_ss.at[slot], agk_rs.at[slot], at(dx, 0, dz, 0))
        cp.start()
        ag.append(cp)
    for cp in r3v:
        cp.wait_recv()
    sum3 = r3v_r[0].astype(F32)
    for j in range(1, 8):
        sum3 = sum3 + r3v_r[j].astype(F32)
    mine_v = x * 4 + yh
    agv_r[mine_v] = sum3.astype(BF)
    for dx, dh in XY:
        slot = dx * 4 + dh
        own = agv_r.at[mine_v]
        cp = remote(own, own, agv_ss.at[slot], agv_rs.at[slot], at(dx, 2 * dh, 0, 0))
        cp.start()
        ag.append(cp)
    krow = lax.broadcasted_iota(jnp.int32, (192, 1024), 0)
    kpos = lax.broadcasted_iota(jnp.int32, (192, 1024), 1)
    kpos = kpos - ((krow // 6) * 32 + lax.rem(krow, 6))
    vrow = lax.broadcasted_iota(jnp.int32, (192, 256), 0)
    vpos = lax.broadcasted_iota(jnp.int32, (192, 256), 1)
    vpos = vpos - ((vrow // 12) * 16 + lax.rem(vrow, 12))
    ksel = [(kpos == 8 * c).astype(F32).astype(BF) for c in range(3)]
    vsel = (vpos == 0).astype(F32).astype(BF)
    for cp in ag:
        cp.wait_recv()
    pieces = agk_r[...].reshape(1024, 128)
    for c in range(3):
        grad_out[:, 128 * c : 128 * c + 128] = mm(ksel[c], pieces).astype(BF)
    grad_out[:, 384:] = mm(vsel, agv_r[...].reshape(256, 384)).astype(BF)
    for cp in dm + late + r2k + r2v + r3k + r3v + ag:
        cp.wait_send()


def per_device(tokens, lengths, partner, w_query, w_keyval, w_output):
    vmem = pl.BlockSpec(memory_space=pltpu.VMEM)
    dma = pltpu.SemaphoreType.DMA
    loss, grad = pl.pallas_call(
        kernel,
        name="contrast",
        out_shape=(
            jax.ShapeDtypeStruct((8, 128), F32),
            jax.ShapeDtypeStruct((192, 768), BF),
        ),
        in_specs=[pl.BlockSpec(memory_space=pl.ANY)] * 5,
        out_specs=(vmem, vmem),
        scratch_shapes=[
            pltpu.SMEM((4,), jnp.int32),
            pltpu.VMEM((640, 768), BF),
            pltpu.VMEM((768, 384), BF),
            pltpu.VMEM((768, 768), BF),
            pltpu.VMEM((384, 768), BF),
            dma((5,)),
            pltpu.VMEM((2, 16, 384), BF),
            pltpu.VMEM((8, 16, 384), BF),
            pltpu.VMEM((8, 8, 16, 768), BF),
            pltpu.VMEM((8, 640, 128), BF),
            pltpu.VMEM((8, 16, 512), BF),
            pltpu.VMEM((8, 16, 512), BF),
            pltpu.VMEM((8, 16, 128), BF),
            pltpu.VMEM((8, 16, 128), BF),
            pltpu.VMEM((16, 384), BF),
            pltpu.VMEM((8, 16, 384), BF),
            pltpu.VMEM((8, 16, 384), BF),
            pltpu.VMEM((8, 16, 384), BF),
            pltpu.VMEM((8, 16, 384), BF),
            pltpu.VMEM((8, 16, 384), BF),
            pltpu.VMEM((2, 32, 128), BF),
            pltpu.VMEM((8, 32, 128), BF),
            pltpu.VMEM((8, 16, 384), BF),
            pltpu.VMEM((32, 32, 128), BF),
            pltpu.VMEM((16, 16, 384), BF),
            pltpu.VMEM((16, 640), F32),
        ]
        + [dma((8,))] * 22
        + [dma((16,))] * 2
        + [dma((32,))] * 2,
        compiler_params=pltpu.CompilerParams(
            collective_id=0, has_side_effects=True, vmem_limit_bytes=107 * 2**19
        ),
    )(jnp.concatenate([lengths, partner]), tokens, w_query, w_keyval, w_output)
    return loss[0, :2], grad.astype(F32)


def solution(mesh):
    in_specs = (P(("col", "rep"), None), P(("col", "rep")), P(("col", "rep")), P(), P(), P())
    out_specs = (P(("col", "rep")), P("rep", None))
    return jax.shard_map(
        per_device, mesh=mesh, in_specs=in_specs, out_specs=out_specs, check_vma=False
    )
```

```python
import functools

import jax
import jax.numpy as jnp
from jax import lax
from jax.experimental import pallas as pl
from jax.experimental.pallas import tpu as pltpu
from jax.sharding import PartitionSpec as P

HEAD = 64
SHARP = 0.07
BF = jnp.bfloat16
F32 = jnp.float32
MESH = pl.DeviceIdType.MESH
NX, NY, NZ = 4, 8, 8
NEAR = (4, 3, 5, 2, 6, 1, 7)


def hops(offset):
    return -sum(min(d, size - d) for d, size in offset)


XC = sorted(
    [(dx, dk) for dx in range(NX) for dk in range(2) if (dx, dk) != (0, 0)],
    key=lambda o: hops([(o[0], NX)]),
)
XZ = sorted(
    [(dx, dz) for dx in range(NX) for dz in range(NZ) if (dx, dz) != (0, 0)],
    key=lambda o: hops([(o[0], NX), (o[1], NZ)]),
)
XY = sorted(
    [(dx, dh) for dx in range(NX) for dh in range(4) if (dx, dh) != (0, 0)],
    key=lambda o: hops([(o[0], NX), (2 * o[1], NY)]),
)
PEERS = sorted(
    {(dx, 0, 0, dk) for dx, dk in XC}
    | {(0, j, 0, 0) for j in NEAR}
    | {(0, 0, j, 0) for j in NEAR}
    | {(dx, 0, dz, 0) for dx, dz in XZ}
    | {(dx, 2 * dh, 0, 0) for dx, dh in XY}
)


def mm(a, b):
    return jnp.dot(a, b, preferred_element_type=F32)


def mm_t(a, b):
    return lax.dot_general(a, b, (((1,), (1,)), ((), ())), preferred_element_type=F32)


def mm_tl(a, b):
    return lax.dot_general(a, b, (((0,), (0,)), ((), ())), preferred_element_type=F32)


def two(a):
    high = a.astype(BF)
    low = (a - high.astype(F32)).astype(BF)
    return jnp.concatenate([high, low], axis=0)


def fold(a):
    return a[:16] + a[16:]


def device(x, y, z, k):
    return ((x * NZ + z) * 4 + y // 2, lax.rem(y, 2) * 2 + k)


def kernel(
    meta_h, tok_h, wq_h, wkv_h, wo_h,
    loss_out, grad_out,
    meta, tok, wq, wkv, wo, in_s,
    a1_s, a1_r, u, tperm, early_s, early_r, late_s, late_r, dm_s, dm_r, r2k_s, r2k_r, r2v_s, r2v_r,
    r3k_s, r3k_r, r3v_r, agk_r, agv_r,
    soft, a1_ss, a1_rs, a2_ss, a2_rs, a3_ss, a3_rs, fw_ss, fw_rs,
    e_ss, e_rs, l_ss, l_rs, d_ss, d_rs, r2k_ss, r2k_rs, r2v_ss, r2v_rs,
    r3k_ss, r3k_rs, r3v_ss, r3v_rs, agv_ss, agv_rs, agk_ss, agk_rs,
):
    col, rep = lax.axis_index("col"), lax.axis_index("rep")
    x, z = col // 32, lax.rem(col // 4, 8)
    yh, yl, k = lax.rem(col, 4), rep // 2, lax.rem(rep, 2)
    y = yh * 2 + yl
    m = x * 2 + k

    def at(dx, dy, dz, dk):
        return (
            lax.rem(x + dx, NX), lax.rem(y + dy, NY), lax.rem(z + dz, NZ), lax.rem(k + dk, 2)
        )

    def remote(src, dst, ss, rs, place):
        return pltpu.make_async_remote_copy(
            src_ref=src, dst_ref=dst, send_sem=ss, recv_sem=rs,
            device_id=device(*place), device_id_type=MESH,
        )

    loads = [
        pltpu.make_async_copy(src, dst, in_s.at[i])
        for i, (src, dst) in enumerate(
            [(meta_h, meta), (tok_h, tok), (wq_h, wq), (wkv_h, wkv), (wo_h, wo)]
        )
    ]
    for cp in loads:
        cp.start()
    barrier = pltpu.get_barrier_semaphore()
    for off in PEERS:
        pl.semaphore_signal(
            barrier, inc=1, device_id=device(*at(*off)), device_id_type=MESH
        )

    row = lax.broadcasted_iota(jnp.int32, (16, 640), 0)
    pos = lax.broadcasted_iota(jnp.int32, (16, 640), 1)
    loads[0].wait()
    loads[1].wait()
    l0, l1 = meta[0], meta[1]
    lo = jnp.where(row < 8, 0, l0)
    hi = jnp.where(row < 8, l0, l0 + l1)
    t = tok[...]
    first = mm((pos == lo).astype(F32).astype(BF), t)
    hrow = lax.rem(lax.broadcasted_iota(jnp.int32, (16, 384), 0), 8)
    own_head = lax.broadcasted_iota(jnp.int32, (16, 384), 1) // HEAD == hrow
    loads[2].wait()
    query = mm(first.astype(BF), wq[...]).astype(BF).astype(F32)
    qexp = jnp.where(own_head, query, 0.0).astype(BF)
    loads[3].wait()
    wk, wv = wkv[:, :384], wkv[:, 384:]
    scores = fold(mm_t(two(mm_t(qexp, wk)), t)) * HEAD ** (-0.5)
    scores = jnp.where((pos >= lo) & (pos < hi), scores, -1e30)
    lifted = jnp.exp(scores - jnp.max(scores, axis=1, keepdims=True))
    weights = lifted / jnp.sum(lifted, axis=1, keepdims=True)
    soft[...] = weights
    wb = weights.astype(BF)
    pooled = mm(wb, t)
    pooled_b = pooled.astype(BF)
    mixed = jnp.where(own_head, fold(mm(two(pooled), wv)), 0.0)
    mixed = jnp.sum(mixed.reshape(2, 8, 384), axis=1, keepdims=True)
    mixed = jnp.broadcast_to(mixed, (2, 8, 384)).reshape(16, 384).astype(BF)
    loads[4].wait()
    embed = first + mm(mixed, wo[...])
    norm = jnp.sqrt(jnp.sum(embed * embed, axis=1, keepdims=True) + 1e-06)
    unit = embed / norm
    unit_b = unit.astype(BF)
    ub = unit_b.astype(F32)
    row16 = lax.broadcasted_iota(jnp.int32, (16, 768), 0)
    placed = jnp.where(row16 == 2 * m, ub[0:1], jnp.where(row16 == 2 * m + 1, ub[8:9], 0.0))
    placed = placed.astype(BF)
    a1_s[0] = placed[:, :384]
    a1_s[1] = placed[:, 384:]

    pl.semaphore_wait(barrier, len(PEERS))

    def group_copies(src, dst, ss, rs):
        copies = []
        for dx, dk in XC:
            place = at(dx, 0, 0, dk)
            slot = dx * 2 + dk
            copies.append(remote(src(place), dst.at[slot], ss.at[slot], rs.at[slot], place))
        return copies

    a1 = group_copies(lambda p: a1_s.at[p[3]], a1_r, a1_ss, a1_rs)
    for cp in a1:
        cp.start()

    lane = lax.broadcasted_iota(jnp.int32, (768, 128), 1)
    deep = lax.broadcasted_iota(jnp.int32, (768, 128), 0)
    part8, pos16, pos8 = lane // 16, lax.rem(lane, 16), lax.rem(lane, 8)
    by_z = jnp.where(pos8 < 6, (pos16 // 8) * 384 + part8 * 6 + pos8, 100000)
    by_y = jnp.where(pos16 < 12, lax.rem(part8, 2) * 384 + (part8 // 2) * 12 + pos16, 100000)

    def pick(base, i):
        return (deep == base + ((i % 2) * 192 + (i // 2) * 48)).astype(F32).astype(BF)

    def permute(i):
        tperm[i] = mm(tok[...], pick(by_z, i)).astype(BF)

    for i in range(2):
        permute(i)
    for cp in a1:
        cp.wait_recv()
    block = a1_s[k].astype(F32)
    for s in range(1, 8):
        block = block + a1_r[s].astype(F32)
    block = block.astype(BF)

    def gather(half):
        lanes = slice(half * 384, half * 384 + 384)
        u[z, y, :, lanes] = block
        mine = u.at[z, y, :, lanes]

        def line(j, second):
            along_z = (half == 0) == second
            return at(0, 0, j, 0) if along_z else at(0, j, 0, 0)

        def plane(j):
            p = at(0, 8 - j, 8 - j, 0)
            return u.at[p[2], :, :, lanes] if half == 0 else u.at[:, p[1], :, lanes]

        own = u.at[z, :, :, lanes] if half == 0 else u.at[:, y, :, lanes]
        a2 = {j: remote(mine, mine, a2_ss.at[j], a2_rs.at[j], line(j, False)) for j in NEAR}
        for j in NEAR:
            a2[j].start()

        def spread(j):
            p = at(0, 8 - j, 8 - j, 0)
            part = u.at[z, p[1], :, lanes] if half == 0 else u.at[p[2], y, :, lanes]
            for d in NEAR:
                remote(part, part, a3_ss.at[d], a3_rs.at[d], line(d, True)).start()

        spread(8)
        for j in reversed(NEAR):
            a2[j].wait_recv()
            spread(j)
        near = NEAR[::-1]
        a3 = [remote(own, own, a3_ss.at[j], a3_rs.at[j], line(j, True)) for j in near]
        fw = []
        for n, j in enumerate((0,) + near):
            if n:
                a3[n - 1].wait_recv()
            reg = own if j == 0 else plane(j)
            cp = remote(reg, reg, fw_ss.at[j], fw_rs.at[j], at(0, 0, 0, 1))
            cp.start()
            fw.append(cp)
            if n == 0:
                for i in range(2, 8):
                    permute(i)
                for i in range(8):
                    early_s[i, :, 0:128] = mm(pooled_b, pick(by_y, i)).astype(BF)
                    early_s[i, :, 128:512] = qexp
                e = group_copies(lambda p: early_s.at[p[0] * 2 + p[3]], early_r, e_ss, e_rs)
                for cp in e:
                    cp.start()
        for cp in fw:
            cp.wait_recv()
        for cp in e:
            cp.wait()

    pl.when(k == 0)(functools.partial(gather, 0))
    pl.when(k == 1)(functools.partial(gather, 1))
    scale = 1.0 / SHARP
    whole = u[...].reshape(1024, 768)
    totals = [jnp.zeros((1, 256), F32)] * 4
    for i in range(4):
        rows = u[2 * i : 2 * i + 2].reshape(256, 768)
        if i == 0:
            rows = jnp.concatenate([rows, unit_b], axis=0)
        block_s = mm_t(rows, u[2 * i :].reshape(1024 - 256 * i, 768)) * scale
        if i == 0:
            logits, block_s = block_s[256:], block_s[:256]
        expd = jnp.exp(block_s)
        down = jnp.sum(expd, axis=0, keepdims=True)
        for j in range(i, 4):
            totals[j] = totals[j] + down[:, 256 * (j - i) : 256 * (j - i) + 256]
        if i < 3:
            ones = jnp.ones((16, 768 - 256 * i), BF)
            totals[i] = totals[i] + mm_t(ones, expd[:, 256:].astype(BF))[0:1]
    all_lse = jnp.log(jnp.concatenate(totals, axis=1))
    lse = jnp.log(jnp.sum(jnp.exp(logits), axis=1, keepdims=True))
    n = lax.broadcasted_iota(jnp.int32, (16, 1024), 1)
    nz, ny, nm, nc = n // 128, lax.rem(n // 16, 8), lax.rem(n // 2, 8), lax.rem(n, 2)
    number = (((nm // 2) * 8 + nz) * 4 + ny // 2) * 4 + lax.rem(ny, 2) * 2 + lax.rem(nm, 2)
    number = number * 2 + nc
    lrow = lax.broadcasted_iota(jnp.int32, (16, 1024), 0)
    match = number == jnp.where(lrow < 8, meta[2], meta[3])
    positive = jnp.sum(jnp.where(match, logits, 0.0), axis=1, keepdims=True)
    loss = lse - positive
    loss_lane = lax.broadcasted_iota(jnp.int32, (8, 128), 1)
    loss_out[...] = jnp.where(loss_lane == 0, loss[0:8], loss[8:16])
    rowp = jnp.exp(logits - lse).astype(BF)
    colp = jnp.exp(logits - all_lse).astype(BF)
    stack = jnp.concatenate([rowp, colp, match.astype(F32).astype(BF)], axis=0)
    terms = mm(stack, whole)
    dunit = (terms[:16] + terms[16:32] - 2.0 * terms[32:]) / SHARP
    radial = jnp.sum(unit * dunit, axis=1, keepdims=True)
    dembed = (dunit - unit * radial) / norm

    dmixed = fold(mm_t(two(dembed), wo[...])).astype(BF).astype(F32)
    dmexp = jnp.where(own_head, dmixed, 0.0).astype(BF)
    dm_s[...] = dmexp
    dm = group_copies(lambda p: dm_s, dm_r, d_ss, d_rs)
    for cp in dm:
        cp.start()
    dm_r[0] = dmexp
    dweights = fold(mm_t(two(mm_t(dmexp, wv)), t)).astype(BF).astype(F32)
    weights = soft[...]
    dscores = weights * (dweights - jnp.sum(weights * dweights, axis=1, keepdims=True))
    ds2 = two(dscores * HEAD ** (-0.5))
    for i in range(8):
        late_s[i] = fold(mm(ds2, tperm[i])).astype(BF)
    late = group_copies(lambda p: late_s.at[p[0] * 2 + p[3]], late_r, l_ss, l_rs)
    for cp in late:
        cp.start()
    early_r[0] = early_s[m]
    late_r[0] = late_s[m]

    r2k, r2v = [], []
    for cp in dm:
        cp.wait_recv()
    vals = mm_tl(early_r[:, :, 0:128].reshape(128, 128), dm_r[...].reshape(128, 384))
    r2v_s[...] = vals.astype(BF).reshape(8, 16, 384)
    for j in NEAR:
        place = at(0, j, 0, 0)
        cp = remote(r2v_s.at[place[1]], r2v_r.at[j], r2v_ss.at[j], r2v_rs.at[j], place)
        cp.start()
        r2v.append(cp)
    for cp in late:
        cp.wait_recv()
    keys = mm_tl(late_r[...].reshape(128, 128), early_r[:, :, 128:512].reshape(128, 384))
    r2k_s[...] = keys.astype(BF).reshape(8, 16, 384)
    for j in NEAR:
        place = at(0, 0, j, 0)
        cp = remote(r2k_s.at[place[2]], r2k_r.at[j], r2k_ss.at[j], r2k_rs.at[j], place)
        cp.start()
        r2k.append(cp)
    r3k, r3v, ag = [], [], []
    sum2 = r2v_s[y].astype(F32)
    for cp, j in zip(r2v, NEAR):
        cp.wait_recv()
        sum2 = sum2 + r2v_r[j].astype(F32)
    r3v_r[z] = sum2.astype(BF)
    for j in NEAR:
        cp = remote(r3v_r.at[z], r3v_r.at[z], r3v_ss.at[j], r3v_rs.at[j], at(0, 0, j, 0))
        cp.start()
        r3v.append(cp)
    sum2 = r2k_s[z].astype(F32)
    for cp, j in zip(r2k, NEAR):
        cp.wait_recv()
        sum2 = sum2 + r2k_r[j].astype(F32)
    for i in range(2):
        half = sum2[8 * i : 8 * i + 8]
        tiles = [half[:, :128], half[:, 128:256], half[:, 256:], jnp.zeros((8, 128), F32)]
        r3k_s[i] = jnp.concatenate(tiles, axis=0).astype(BF)
    for j in NEAR:
        place = at(0, j, 0, 0)
        src = r3k_s.at[lax.rem(place[1], 2)]
        cp = remote(src, r3k_r.at[y], r3k_ss.at[j], r3k_rs.at[j], place)
        cp.start()
        r3k.append(cp)
    r3k_r[y] = r3k_s[yl]

    for cp in r3v:
        cp.wait_recv()
    sum3 = r3v_r[0].astype(F32)
    for j in range(1, 8):
        sum3 = sum3 + r3v_r[j].astype(F32)
    mine_v = x * 4 + yh
    agv_r[mine_v] = sum3.astype(BF)
    for dx, dh in XY:
        slot = dx * 4 + dh
        own = agv_r.at[mine_v]
        cp = remote(own, own, agv_ss.at[slot], agv_rs.at[slot], at(dx, 2 * dh, 0, 0))
        cp.start()
        ag.append(cp)
    for cp in r3k:
        cp.wait_recv()
    sum3 = r3k_r[0].astype(F32)
    for j in range(1, 8):
        sum3 = sum3 + r3k_r[j].astype(F32)
    mine = x * 8 + z
    agk_r[mine] = sum3.astype(BF)
    for dx, dz in XZ:
        slot = dx * 8 + dz
        own = agk_r.at[mine]
        cp = remote(own, own, agk_ss.at[slot], agk_rs.at[slot], at(dx, 0, dz, 0))
        cp.start()
        ag.append(cp)
    krow = lax.broadcasted_iota(jnp.int32, (192, 1024), 0)
    kpos = lax.broadcasted_iota(jnp.int32, (192, 1024), 1)
    kpos = kpos - ((krow // 6) * 32 + lax.rem(krow, 6))
    vrow = lax.broadcasted_iota(jnp.int32, (192, 256), 0)
    vpos = lax.broadcasted_iota(jnp.int32, (192, 256), 1)
    vpos = vpos - ((vrow // 12) * 16 + lax.rem(vrow, 12))
    ksel = [(kpos == 8 * c).astype(F32).astype(BF) for c in range(3)]
    vsel = (vpos == 0).astype(F32).astype(BF)
    for cp in ag:
        cp.wait_recv()
    pieces = agk_r[...].reshape(1024, 128)
    for c in range(3):
        grad_out[:, 128 * c : 128 * c + 128] = mm(ksel[c], pieces).astype(BF)
    grad_out[:, 384:] = mm(vsel, agv_r[...].reshape(256, 384)).astype(BF)
    one, eight = u.at[0, 0, :, 0:384], u.at[0, :, :, 0:384]
    for j in NEAR:
        remote(one, one, a2_ss.at[j], a2_rs.at[j], at(0, j, 0, 0)).wait_send()
        remote(eight, eight, a3_ss.at[j], a3_rs.at[j], at(0, j, 0, 0)).wait_send()
    for j in range(8):
        remote(eight, eight, fw_ss.at[j], fw_rs.at[j], at(0, 0, 0, 1)).wait_send()
    for cp in a1 + dm + late + r2k + r2v + r3k + r3v + ag:
        cp.wait_send()


def per_device(tokens, lengths, partner, w_query, w_keyval, w_output):
    vmem = pl.BlockSpec(memory_space=pltpu.VMEM)
    dma = pltpu.SemaphoreType.DMA
    loss, grad = pl.pallas_call(
        kernel,
        name="contrast",
        out_shape=(
            jax.ShapeDtypeStruct((8, 128), F32),
            jax.ShapeDtypeStruct((192, 768), BF),
        ),
        in_specs=[pl.BlockSpec(memory_space=pl.ANY)] * 5,
        out_specs=(vmem, vmem),
        scratch_shapes=[
            pltpu.SMEM((4,), jnp.int32),
            pltpu.VMEM((640, 768), BF),
            pltpu.VMEM((768, 384), BF),
            pltpu.VMEM((768, 768), BF),
            pltpu.VMEM((384, 768), BF),
            dma((5,)),
            pltpu.VMEM((2, 16, 384), BF),
            pltpu.VMEM((8, 16, 384), BF),
            pltpu.VMEM((8, 8, 16, 768), BF),
            pltpu.VMEM((8, 640, 128), BF),
            pltpu.VMEM((8, 16, 512), BF),
            pltpu.VMEM((8, 16, 512), BF),
            pltpu.VMEM((8, 16, 128), BF),
            pltpu.VMEM((8, 16, 128), BF),
            pltpu.VMEM((16, 384), BF),
            pltpu.VMEM((8, 16, 384), BF),
            pltpu.VMEM((8, 16, 384), BF),
            pltpu.VMEM((8, 16, 384), BF),
            pltpu.VMEM((8, 16, 384), BF),
            pltpu.VMEM((8, 16, 384), BF),
            pltpu.VMEM((2, 32, 128), BF),
            pltpu.VMEM((8, 32, 128), BF),
            pltpu.VMEM((8, 16, 384), BF),
            pltpu.VMEM((32, 32, 128), BF),
            pltpu.VMEM((16, 16, 384), BF),
            pltpu.VMEM((16, 640), F32),
        ]
        + [dma((8,))] * 22
        + [dma((16,))] * 2
        + [dma((32,))] * 2,
        compiler_params=pltpu.CompilerParams(
            collective_id=0, has_side_effects=True, vmem_limit_bytes=107 * 2**19
        ),
    )(jnp.concatenate([lengths, partner]), tokens, w_query, w_keyval, w_output)
    return loss[0, :2], grad.astype(F32)


def solution(mesh):
    in_specs = (P(("col", "rep"), None), P(("col", "rep")), P(("col", "rep")), P(), P(), P())
    out_specs = (P(("col", "rep")), P("rep", None))
    return jax.shard_map(
        per_device, mesh=mesh, in_specs=in_specs, out_specs=out_specs, check_vma=False
    )
```

```python
import functools

import jax
import jax.numpy as jnp
from jax import lax
from jax.experimental import pallas as pl
from jax.experimental.pallas import tpu as pltpu
from jax.sharding import PartitionSpec as P

HEAD = 64
SHARP = 0.07
BF = jnp.bfloat16
F32 = jnp.float32
MESH = pl.DeviceIdType.MESH
NX, NY, NZ = 4, 8, 8
NEAR = (4, 3, 5, 2, 6, 1, 7)


def hops(offset):
    return -sum(min(d, size - d) for d, size in offset)


XC = sorted(
    [(dx, dk) for dx in range(NX) for dk in range(2) if (dx, dk) != (0, 0)],
    key=lambda o: hops([(o[0], NX)]),
)
XZ = sorted(
    [(dx, dz) for dx in range(NX) for dz in range(NZ) if (dx, dz) != (0, 0)],
    key=lambda o: hops([(o[0], NX), (o[1], NZ)]),
)
XY = sorted(
    [(dx, dh) for dx in range(NX) for dh in range(4) if (dx, dh) != (0, 0)],
    key=lambda o: hops([(o[0], NX), (2 * o[1], NY)]),
)
PEERS = sorted(
    {(dx, 0, 0, dk) for dx, dk in XC}
    | {(0, j, 0, 0) for j in NEAR}
    | {(0, 0, j, 0) for j in NEAR}
    | {(dx, 0, dz, 0) for dx, dz in XZ}
    | {(dx, 2 * dh, 0, 0) for dx, dh in XY}
)


def mm(a, b):
    return jnp.dot(a, b, preferred_element_type=F32)


def mm_t(a, b):
    return lax.dot_general(a, b, (((1,), (1,)), ((), ())), preferred_element_type=F32)


def mm_tl(a, b):
    return lax.dot_general(a, b, (((0,), (0,)), ((), ())), preferred_element_type=F32)


def two(a):
    high = a.astype(BF)
    low = (a - high.astype(F32)).astype(BF)
    return jnp.concatenate([high, low], axis=0)


def fold(a):
    return a[:16] + a[16:]


def device(x, y, z, k):
    return ((x * NZ + z) * 4 + y // 2, lax.rem(y, 2) * 2 + k)


def kernel(
    meta_h, tok_h, wq_h, wkv_h, wo_h,
    loss_out, grad_out,
    meta, tok, wq, wkv, wo, in_s,
    a1_s, a1_r, u, tperm, early_s, early_r, late_s, late_r, dm_s, dm_r, r2k_s, r2k_r, r2v_s, r2v_r,
    r3k_s, r3k_r, r3v_r, agk_r, agv_r,
    soft, a1_ss, a1_rs, a2_ss, a2_rs, a3_ss, a3_rs, fw_ss, fw_rs,
    e_ss, e_rs, l_ss, l_rs, d_ss, d_rs, r2k_ss, r2k_rs, r2v_ss, r2v_rs,
    r3k_ss, r3k_rs, r3v_ss, r3v_rs, agv_ss, agv_rs, agk_ss, agk_rs,
):
    col, rep = lax.axis_index("col"), lax.axis_index("rep")
    x, z = col // 32, lax.rem(col // 4, 8)
    yh, yl, k = lax.rem(col, 4), rep // 2, lax.rem(rep, 2)
    y = yh * 2 + yl
    m = x * 2 + k

    def at(dx, dy, dz, dk):
        return (
            lax.rem(x + dx, NX), lax.rem(y + dy, NY), lax.rem(z + dz, NZ), lax.rem(k + dk, 2)
        )

    def remote(src, dst, ss, rs, place):
        return pltpu.make_async_remote_copy(
            src_ref=src, dst_ref=dst, send_sem=ss, recv_sem=rs,
            device_id=device(*place), device_id_type=MESH,
        )

    parts = [(meta_h, meta)]
    parts += [(tok_h.at[160 * i : 160 * i + 160], tok.at[160 * i : 160 * i + 160]) for i in range(4)]
    parts += [(wq_h, wq), (wkv_h.at[:, 0:384], wkv.at[:, 0:384])]
    parts += [(wkv_h.at[:, 384:768], wkv.at[:, 384:768]), (wo_h, wo)]
    loads = [pltpu.make_async_copy(src, dst, in_s.at[i]) for i, (src, dst) in enumerate(parts)]
    for cp in loads[:7]:
        cp.start()
    barrier = pltpu.get_barrier_semaphore()
    for off in PEERS:
        pl.semaphore_signal(
            barrier, inc=1, device_id=device(*at(*off)), device_id_type=MESH
        )

    row = lax.broadcasted_iota(jnp.int32, (16, 640), 0)
    pos = lax.broadcasted_iota(jnp.int32, (16, 640), 1)
    for cp in loads[:5]:
        cp.wait()
    for cp in loads[7:]:
        cp.start()
    l0, l1 = meta[0], meta[1]
    lo = jnp.where(row < 8, 0, l0)
    hi = jnp.where(row < 8, l0, l0 + l1)
    t = tok[...]
    first = mm((pos == lo).astype(F32).astype(BF), t)
    hrow = lax.rem(lax.broadcasted_iota(jnp.int32, (16, 384), 0), 8)
    own_head = lax.broadcasted_iota(jnp.int32, (16, 384), 1) // HEAD == hrow
    loads[5].wait()
    query = mm(first.astype(BF), wq[...]).astype(BF).astype(F32)
    qexp = jnp.where(own_head, query, 0.0).astype(BF)
    loads[6].wait()
    wk = wkv[:, :384]
    scores = fold(mm_t(two(mm_t(qexp, wk)), t)) * HEAD ** (-0.5)
    scores = jnp.where((pos >= lo) & (pos < hi), scores, -1e30)
    lifted = jnp.exp(scores - jnp.max(scores, axis=1, keepdims=True))
    weights = lifted / jnp.sum(lifted, axis=1, keepdims=True)
    soft[...] = weights
    wb = weights.astype(BF)
    pooled = mm(wb, t)
    pooled_b = pooled.astype(BF)
    loads[7].wait()
    wv = wkv[:, 384:]
    mixed = jnp.where(own_head, fold(mm(two(pooled), wv)), 0.0)
    mixed = jnp.sum(mixed.reshape(2, 8, 384), axis=1, keepdims=True)
    mixed = jnp.broadcast_to(mixed, (2, 8, 384)).reshape(16, 384).astype(BF)
    loads[8].wait()
    embed = first + mm(mixed, wo[...])
    norm = jnp.sqrt(jnp.sum(embed * embed, axis=1, keepdims=True) + 1e-06)
    unit = embed / norm
    unit_b = unit.astype(BF)
    ub = unit_b.astype(F32)
    row16 = lax.broadcasted_iota(jnp.int32, (16, 768), 0)
    placed = jnp.where(row16 == 2 * m, ub[0:1], jnp.where(row16 == 2 * m + 1, ub[8:9], 0.0))
    placed = placed.astype(BF)
    a1_s[0] = placed[:, :384]
    a1_s[1] = placed[:, 384:]

    pl.semaphore_wait(barrier, len(PEERS))

    def group_copies(src, dst, ss, rs):
        copies = []
        for dx, dk in XC:
            place = at(dx, 0, 0, dk)
            slot = dx * 2 + dk
            copies.append(remote(src(place), dst.at[slot], ss.at[slot], rs.at[slot], place))
        return copies

    a1 = group_copies(lambda p: a1_s.at[p[3]], a1_r, a1_ss, a1_rs)
    for cp in a1:
        cp.start()

    lane = lax.broadcasted_iota(jnp.int32, (768, 128), 1)
    deep = lax.broadcasted_iota(jnp.int32, (768, 128), 0)
    part8, pos16, pos8 = lane // 16, lax.rem(lane, 16), lax.rem(lane, 8)
    by_z = jnp.where(pos8 < 6, (pos16 // 8) * 384 + part8 * 6 + pos8, 100000)
    by_y = jnp.where(pos16 < 12, lax.rem(part8, 2) * 384 + (part8 // 2) * 12 + pos16, 100000)

    def pick(base, i):
        return (deep == base + ((i % 2) * 192 + (i // 2) * 48)).astype(F32).astype(BF)

    def permute(i):
        tperm[i] = mm(tok[...], pick(by_z, i)).astype(BF)

    for i in range(2):
        permute(i)
    for cp in a1:
        cp.wait_recv()
    block = a1_s[k].astype(F32)
    for s in range(1, 8):
        block = block + a1_r[s].astype(F32)
    block = block.astype(BF)

    def gather(half):
        lanes = slice(half * 384, half * 384 + 384)
        u[z, y, :, lanes] = block
        mine = u.at[z, y, :, lanes]

        def line(j, second):
            along_z = (half == 0) == second
            return at(0, 0, j, 0) if along_z else at(0, j, 0, 0)

        def plane(j):
            p = at(0, 8 - j, 8 - j, 0)
            return u.at[p[2], :, :, lanes] if half == 0 else u.at[:, p[1], :, lanes]

        own = u.at[z, :, :, lanes] if half == 0 else u.at[:, y, :, lanes]
        a2 = {j: remote(mine, mine, a2_ss.at[j], a2_rs.at[j], line(j, False)) for j in NEAR}
        for j in NEAR:
            a2[j].start()

        def spread(j):
            p = at(0, 8 - j, 8 - j, 0)
            part = u.at[z, p[1], :, lanes] if half == 0 else u.at[p[2], y, :, lanes]
            for d in NEAR:
                remote(part, part, a3_ss.at[d], a3_rs.at[d], line(d, True)).start()

        spread(8)
        for j in reversed(NEAR):
            a2[j].wait_recv()
            spread(j)
        near = NEAR[::-1]
        a3 = [remote(own, own, a3_ss.at[j], a3_rs.at[j], line(j, True)) for j in near]
        fw = []
        for n, j in enumerate((0,) + near):
            if n:
                a3[n - 1].wait_recv()
            reg = own if j == 0 else plane(j)
            cp = remote(reg, reg, fw_ss.at[j], fw_rs.at[j], at(0, 0, 0, 1))
            cp.start()
            fw.append(cp)
            if n == 0:
                for i in range(2, 8):
                    permute(i)
                for i in range(8):
                    early_s[i, :, 0:128] = mm(pooled_b, pick(by_y, i)).astype(BF)
                    early_s[i, :, 128:512] = qexp
                e = group_copies(lambda p: early_s.at[p[0] * 2 + p[3]], early_r, e_ss, e_rs)
                for cp in e:
                    cp.start()
        for cp in fw:
            cp.wait_recv()
        for cp in e:
            cp.wait()

    pl.when(k == 0)(functools.partial(gather, 0))
    pl.when(k == 1)(functools.partial(gather, 1))
    scale = 1.0 / SHARP
    whole = u[...].reshape(1024, 768)
    totals = [jnp.zeros((1, 256), F32)] * 4
    for i in range(4):
        rows = u[2 * i : 2 * i + 2].reshape(256, 768)
        if i == 0:
            rows = jnp.concatenate([rows, unit_b], axis=0)
        block_s = mm_t(rows, u[2 * i :].reshape(1024 - 256 * i, 768)) * scale
        if i == 0:
            logits, block_s = block_s[256:], block_s[:256]
        expd = jnp.exp(block_s)
        down = jnp.sum(expd, axis=0, keepdims=True)
        for j in range(i, 4):
            totals[j] = totals[j] + down[:, 256 * (j - i) : 256 * (j - i) + 256]
        if i < 3:
            ones = jnp.ones((16, 768 - 256 * i), BF)
            totals[i] = totals[i] + mm_t(ones, expd[:, 256:].astype(BF))[0:1]
    all_lse = jnp.log(jnp.concatenate(totals, axis=1))
    lse = jnp.log(jnp.sum(jnp.exp(logits), axis=1, keepdims=True))
    n = lax.broadcasted_iota(jnp.int32, (16, 1024), 1)
    nz, ny, nm, nc = n // 128, lax.rem(n // 16, 8), lax.rem(n // 2, 8), lax.rem(n, 2)
    number = (((nm // 2) * 8 + nz) * 4 + ny // 2) * 4 + lax.rem(ny, 2) * 2 + lax.rem(nm, 2)
    number = number * 2 + nc
    lrow = lax.broadcasted_iota(jnp.int32, (16, 1024), 0)
    match = number == jnp.where(lrow < 8, meta[2], meta[3])
    positive = jnp.sum(jnp.where(match, logits, 0.0), axis=1, keepdims=True)
    loss = lse - positive
    loss_lane = lax.broadcasted_iota(jnp.int32, (8, 128), 1)
    loss_out[...] = jnp.where(loss_lane == 0, loss[0:8], loss[8:16])
    rowp = jnp.exp(logits - lse).astype(BF)
    colp = jnp.exp(logits - all_lse).astype(BF)
    stack = jnp.concatenate([rowp, colp, match.astype(F32).astype(BF)], axis=0)
    terms = mm(stack, whole)
    dunit = (terms[:16] + terms[16:32] - 2.0 * terms[32:]) / SHARP
    radial = jnp.sum(unit * dunit, axis=1, keepdims=True)
    dembed = (dunit - unit * radial) / norm

    dmixed = fold(mm_t(two(dembed), wo[...])).astype(BF).astype(F32)
    dmexp = jnp.where(own_head, dmixed, 0.0).astype(BF)
    dm_s[...] = dmexp
    dm = group_copies(lambda p: dm_s, dm_r, d_ss, d_rs)
    for cp in dm:
        cp.start()
    dm_r[0] = dmexp
    dweights = fold(mm_t(two(mm_t(dmexp, wv)), t)).astype(BF).astype(F32)
    weights = soft[...]
    dscores = weights * (dweights - jnp.sum(weights * dweights, axis=1, keepdims=True))
    ds2 = two(dscores * HEAD ** (-0.5))
    for i in range(8):
        late_s[i] = fold(mm(ds2, tperm[i])).astype(BF)
    late = group_copies(lambda p: late_s.at[p[0] * 2 + p[3]], late_r, l_ss, l_rs)
    for cp in late:
        cp.start()
    early_r[0] = early_s[m]
    late_r[0] = late_s[m]

    r2k, r2v = [], []
    for cp in dm:
        cp.wait_recv()
    vals = mm_tl(early_r[:, :, 0:128].reshape(128, 128), dm_r[...].reshape(128, 384))
    r2v_s[...] = vals.astype(BF).reshape(8, 16, 384)
    for j in NEAR:
        place = at(0, j, 0, 0)
        cp = remote(r2v_s.at[place[1]], r2v_r.at[j], r2v_ss.at[j], r2v_rs.at[j], place)
        cp.start()
        r2v.append(cp)
    for cp in late:
        cp.wait_recv()
    keys = mm_tl(late_r[...].reshape(128, 128), early_r[:, :, 128:512].reshape(128, 384))
    r2k_s[...] = keys.astype(BF).reshape(8, 16, 384)
    for j in NEAR:
        place = at(0, 0, j, 0)
        cp = remote(r2k_s.at[place[2]], r2k_r.at[j], r2k_ss.at[j], r2k_rs.at[j], place)
        cp.start()
        r2k.append(cp)
    r3k, r3v, ag = [], [], []
    sum2 = r2v_s[y].astype(F32)
    for cp, j in zip(r2v, NEAR):
        cp.wait_recv()
        sum2 = sum2 + r2v_r[j].astype(F32)
    r3v_r[z] = sum2.astype(BF)
    for j in NEAR:
        cp = remote(r3v_r.at[z], r3v_r.at[z], r3v_ss.at[j], r3v_rs.at[j], at(0, 0, j, 0))
        cp.start()
        r3v.append(cp)
    sum2 = r2k_s[z].astype(F32)
    for cp, j in zip(r2k, NEAR):
        cp.wait_recv()
        sum2 = sum2 + r2k_r[j].astype(F32)
    for i in range(2):
        half = sum2[8 * i : 8 * i + 8]
        tiles = [half[:, :128], half[:, 128:256], half[:, 256:], jnp.zeros((8, 128), F32)]
        r3k_s[i] = jnp.concatenate(tiles, axis=0).astype(BF)
    for j in NEAR:
        place = at(0, j, 0, 0)
        src = r3k_s.at[lax.rem(place[1], 2)]
        cp = remote(src, r3k_r.at[y], r3k_ss.at[j], r3k_rs.at[j], place)
        cp.start()
        r3k.append(cp)
    r3k_r[y] = r3k_s[yl]

    for cp in r3v:
        cp.wait_recv()
    sum3 = r3v_r[0].astype(F32)
    for j in range(1, 8):
        sum3 = sum3 + r3v_r[j].astype(F32)
    mine_v = x * 4 + yh
    agv_r[mine_v] = sum3.astype(BF)
    for dx, dh in XY:
        slot = dx * 4 + dh
        own = agv_r.at[mine_v]
        cp = remote(own, own, agv_ss.at[slot], agv_rs.at[slot], at(dx, 2 * dh, 0, 0))
        cp.start()
        ag.append(cp)
    for cp in r3k:
        cp.wait_recv()
    sum3 = r3k_r[0].astype(F32)
    for j in range(1, 8):
        sum3 = sum3 + r3k_r[j].astype(F32)
    mine = x * 8 + z
    agk_r[mine] = sum3.astype(BF)
    for dx, dz in XZ:
        slot = dx * 8 + dz
        own = agk_r.at[mine]
        cp = remote(own, own, agk_ss.at[slot], agk_rs.at[slot], at(dx, 0, dz, 0))
        cp.start()
        ag.append(cp)
    krow = lax.broadcasted_iota(jnp.int32, (192, 1024), 0)
    kpos = lax.broadcasted_iota(jnp.int32, (192, 1024), 1)
    kpos = kpos - ((krow // 6) * 32 + lax.rem(krow, 6))
    vrow = lax.broadcasted_iota(jnp.int32, (192, 256), 0)
    vpos = lax.broadcasted_iota(jnp.int32, (192, 256), 1)
    vpos = vpos - ((vrow // 12) * 16 + lax.rem(vrow, 12))
    ksel = [(kpos == 8 * c).astype(F32).astype(BF) for c in range(3)]
    vsel = (vpos == 0).astype(F32).astype(BF)
    for cp in ag:
        cp.wait_recv()
    pieces = agk_r[...].reshape(1024, 128)
    for c in range(3):
        grad_out[:, 128 * c : 128 * c + 128] = mm(ksel[c], pieces).astype(BF)
    grad_out[:, 384:] = mm(vsel, agv_r[...].reshape(256, 384)).astype(BF)
    one, eight = u.at[0, 0, :, 0:384], u.at[0, :, :, 0:384]
    for j in NEAR:
        remote(one, one, a2_ss.at[j], a2_rs.at[j], at(0, j, 0, 0)).wait_send()
        remote(eight, eight, a3_ss.at[j], a3_rs.at[j], at(0, j, 0, 0)).wait_send()
    for j in range(8):
        remote(eight, eight, fw_ss.at[j], fw_rs.at[j], at(0, 0, 0, 1)).wait_send()
    for cp in a1 + dm + late + r2k + r2v + r3k + r3v + ag:
        cp.wait_send()


def per_device(tokens, lengths, partner, w_query, w_keyval, w_output):
    vmem = pl.BlockSpec(memory_space=pltpu.VMEM)
    dma = pltpu.SemaphoreType.DMA
    loss, grad = pl.pallas_call(
        kernel,
        name="contrast",
        out_shape=(
            jax.ShapeDtypeStruct((8, 128), F32),
            jax.ShapeDtypeStruct((192, 768), BF),
        ),
        in_specs=[pl.BlockSpec(memory_space=pl.ANY)] * 5,
        out_specs=(vmem, vmem),
        scratch_shapes=[
            pltpu.SMEM((4,), jnp.int32),
            pltpu.VMEM((640, 768), BF),
            pltpu.VMEM((768, 384), BF),
            pltpu.VMEM((768, 768), BF),
            pltpu.VMEM((384, 768), BF),
            dma((9,)),
            pltpu.VMEM((2, 16, 384), BF),
            pltpu.VMEM((8, 16, 384), BF),
            pltpu.VMEM((8, 8, 16, 768), BF),
            pltpu.VMEM((8, 640, 128), BF),
            pltpu.VMEM((8, 16, 512), BF),
            pltpu.VMEM((8, 16, 512), BF),
            pltpu.VMEM((8, 16, 128), BF),
            pltpu.VMEM((8, 16, 128), BF),
            pltpu.VMEM((16, 384), BF),
            pltpu.VMEM((8, 16, 384), BF),
            pltpu.VMEM((8, 16, 384), BF),
            pltpu.VMEM((8, 16, 384), BF),
            pltpu.VMEM((8, 16, 384), BF),
            pltpu.VMEM((8, 16, 384), BF),
            pltpu.VMEM((2, 32, 128), BF),
            pltpu.VMEM((8, 32, 128), BF),
            pltpu.VMEM((8, 16, 384), BF),
            pltpu.VMEM((32, 32, 128), BF),
            pltpu.VMEM((16, 16, 384), BF),
            pltpu.VMEM((16, 640), F32),
        ]
        + [dma((8,))] * 22
        + [dma((16,))] * 2
        + [dma((32,))] * 2,
        compiler_params=pltpu.CompilerParams(
            collective_id=0, has_side_effects=True, vmem_limit_bytes=107 * 2**19
        ),
    )(jnp.concatenate([lengths, partner]), tokens, w_query, w_keyval, w_output)
    return loss[0, :2], grad.astype(F32)


def solution(mesh):
    in_specs = (P(("col", "rep"), None), P(("col", "rep")), P(("col", "rep")), P(), P(), P())
    out_specs = (P(("col", "rep")), P("rep", None))
    return jax.shard_map(
        per_device, mesh=mesh, in_specs=in_specs, out_specs=out_specs, check_vma=False
    )
```
